512 devices in a mesh: band: 4 (over x), group: 16 (over z), patch: 8 (over y, core).
Axes of the slice: x: 4, y: 4, z: 16, core: 2. Of those that a mesh axis runs over, the one named last changes fastest.
Arguments:
- tile_flux: bfloat16 [4, 1024, 128, 128], P('band', ('group', 'patch')), may hold values from -6 to 6
- inverse_var: bfloat16 [4, 1024, 128, 128], P('band', ('group', 'patch')), may hold values from 0.25 to 4
- kernel_coef: bfloat16 [4, 1024, 27], P('band', ('group', 'patch')), may hold values from -4 to 4
- owner_index: int32 [4, 1024, 1], P('band', ('group', 'patch')), may hold values from 0 to 7; in each aligned block of 8 rows (0 to 7, 8 to 15, ..., all dimensions but the last counted through in order) at most 2 rows name the same one
- offsets: int32 [4, 1024, 2], P('band', ('group', 'patch')), may hold values from 0 to 48
- pad_widths: int32 [4, 1024, 4], P('band', ('group', 'patch')), may hold values from 0 to 32
Outputs:
- coadd: float32 [4, 8, 512, 512], P('band', 'patch', 'group')
- chi_square: float32 [8, 512, 512], P('patch', 'group')
The draws below stay inside these ranges and needn't reach their ends.
Inputs may be any that keep to these rules, and one draw needn't show every extreme that they name: `owner_index`: among the 8 tiles of one device (an aligned block of rows of a band), no patch is named more than 2 times, a bound that some block reaches.
All inputs are finite; a program needn't handle non-finite values.
Results may differ from the reference program's by a relative error of at most 0.0044.
Values may be sent and summed in bfloat16 or wider, within the bound.
No kernel may reach another device: no remote copies, remote signals or barrier semaphores. Data moves between devices by JAX's collectives and lax.ppermute only.
A program may use at most 64 MiB of HBM per device.

```python
import math
import jax
import jax.numpy as jnp
import numpy as np
from jax import lax

TILE = 128
PATCH_SIDE = 512
TERMS = 27
TILES_DEV = 8
BANDS = 4
PATCHES = 8
CAP = 2
EXPOSURE_TILES = 1024
N_PATCH = 8


def place_ends(values, key, low, largest):
    longest = values.shape.index(max(values.shape))
    spots = []
    for shift in (0, 1):
        where = [jax.random.randint(jax.random.fold_in(key, axis), (), 0, length) for axis, length in enumerate(values.shape)]
        where[longest] = (where[longest] + shift) % values.shape[longest]
        spots.append(tuple(where))
    return values.at[spots[0]].set(low).at[spots[1]].set(largest)


def block_scale(key, extent, cuts, low, largest):
    factor_of, own = 1.0, jax.random.fold_in(key, 6)
    for axis_at, shards_of in cuts:
        heights = jnp.exp(jax.random.uniform(jax.random.fold_in(own, axis_at), (shards_of,), jnp.float32, low / len(cuts), largest / len(cuts)))
        factor_of = factor_of * jnp.repeat(heights, extent[axis_at] // shards_of).reshape([-1 if axis == axis_at else 1 for axis in range(len(extent))])
    return factor_of


def deal_out(key, own, number, rows, number_of, top, bound, skew):
    ranking = jax.random.permutation(key, number_of)
    packed, ordinary = shares(number_of, rows * top, bound, skew, True), shares(number_of, rows * top, bound, skew, False)
    places = jnp.arange(number_of)

    def named(tallies, offset_by):
        used = int((tallies > 0).sum())
        fixed = max(1, used // 4)
        shifted = fixed + (places - fixed + offset_by * (used - fixed)) % max(1, number_of - fixed)
        return jnp.zeros((number_of,), jnp.int32).at[ranking[jnp.where(places < fixed, places, shifted)]].set(jnp.asarray(tallies, jnp.int32))

    tallies = jnp.where(number % 4 == 0, named(packed, number // 4), named(ordinary, number - number // 4 - 1))
    mixed = jax.random.permutation(jax.random.fold_in(own, 3), number_of)
    giver, receiver = mixed[0:number_of // 2 * 2:2], mixed[1:number_of // 2 * 2:2]
    slack = jnp.minimum(tallies[giver] - 1, bound - tallies[receiver]) // 2
    slack = jnp.where((giver == ranking[0]) | (receiver == ranking[0]) | (tallies[receiver] == 0), 0, jnp.maximum(slack, 0))
    shifted = jax.random.randint(jax.random.fold_in(own, 4), (number_of // 2,), 0, 1 << 20) % (slack + 1)
    tallies = tallies.at[giver].add(-shifted).at[receiver].add(shifted)
    members = jnp.searchsorted(jnp.cumsum(tallies), jnp.arange(rows * top), side="right").astype(jnp.int32)
    grid = members.reshape(top, rows).T
    grid = grid[jax.random.permutation(jax.random.fold_in(own, 1), rows)]
    offset_by = jax.random.randint(jax.random.fold_in(own, 2), (rows, 1), 0, top)
    return jnp.take_along_axis(grid, (jnp.arange(top)[None, :] + offset_by) % top, axis=1)


def shares(number_of, total, limit, skew, full):
    loads = [(1 << 20) // math.isqrt(standing ** skew) + 1 for standing in range(1, number_of + 1)]
    largest = limit if full else min(limit, max(-(-total // number_of), total * loads[0] // sum(loads)))
    least = 1 if total - largest >= number_of - 1 else 0
    given, spare = [largest] + [least] * (number_of - 1), total - largest - least * (number_of - 1)
    while spare > 0:
        movable = [i for i in range(1, number_of) if given[i] < largest] or [i for i in range(1, number_of) if given[i] < limit]
        whole, budget = sum([loads[i] for i in movable]), spare
        for i in movable:
            more = min(limit - given[i], max(1, budget * loads[i] // whole), spare)
            given[i] = given[i] + more
            spare = spare - more
    return np.array(given)


def centred(stream_key, shape, width, most, pieces=(), held_as=jnp.bfloat16):
    gain = block_scale(stream_key, shape, pieces, -0.22, 0.18) if pieces else 1.0
    values = jax.random.normal(stream_key, shape, jnp.float32) * width * gain
    return jnp.minimum(jnp.maximum(values, -most), most).astype(held_as)


def setup_inputs(seed: int = 0) -> dict:
    key_list = jax.random.split(jax.random.key(seed), 7)
    tile_flux = centred(key_list[0], (BANDS, EXPOSURE_TILES, TILE, TILE), 1.0, 6.0, ((0, 4), (1, 128)))
    inverse_var = jnp.clip(jnp.exp(math.log(4.0) - 2.7725887 * jax.random.uniform(key_list[1], (BANDS, EXPOSURE_TILES, TILE, TILE), jnp.float32) ** block_scale(key_list[1], (BANDS, EXPOSURE_TILES, TILE, TILE), ((0, 4), (1, 128)), -0.2, 0.2)), 0.25, 4.0).astype(jnp.bfloat16)
    kernel_coef = centred(key_list[2], (BANDS, EXPOSURE_TILES, TERMS), 1.0, 4.0, ((0, 4), (1, 128)))
    owner_index_keys = jax.random.split(jax.random.fold_in(key_list[3], 1), BANDS * EXPOSURE_TILES // TILES_DEV)
    owner_index_turns = jax.random.permutation(jax.random.fold_in(key_list[3], 3), BANDS * EXPOSURE_TILES // TILES_DEV)
    owner_index = jax.vmap(lambda own, number: deal_out(jax.random.fold_in(key_list[3], 2), own, number, TILES_DEV, N_PATCH, 1, CAP, 2))(owner_index_keys, owner_index_turns).reshape((BANDS, EXPOSURE_TILES, 1))
    offsets = place_ends(jax.random.randint(key_list[4], (BANDS, EXPOSURE_TILES, 2), 0, (PATCH_SIDE - TILE) // 8 + 1), jax.random.fold_in(key_list[4], 1), 0, ((PATCH_SIDE - TILE) // 8 + 1) - 1).astype(jnp.int32)
    pad_widths = place_ends(jax.random.randint(key_list[5], (BANDS, EXPOSURE_TILES, 4), 0, TILE // 4 + 1), jax.random.fold_in(key_list[5], 1), 0, (TILE // 4 + 1) - 1).astype(jnp.int32)
    return dict(tile_flux=tile_flux, inverse_var=inverse_var, kernel_coef=kernel_coef, owner_index=owner_index, offsets=offsets, pad_widths=pad_widths)


SPREADS = (0.7, 1.5, 3.0)
DEGREES = (4, 2, 2)
REACH = 10


def basis_filters():
    offsets_axis = np.arange(-REACH, REACH + 1) * 1.0
    filters = []
    for spread_value, degree in zip(SPREADS, DEGREES):
        profile = np.exp(-offsets_axis ** 2 / (2.0 * spread_value * spread_value))
        profile = profile / profile.sum()
        for exponent in range(degree + 1):
            filters.append(profile * (offsets_axis / REACH) ** exponent)
    return np.stack(filters)


def term_table():
    starts = np.cumsum([0] + [degree + 1 for degree in DEGREES])
    filter_count = int(starts[-1])
    term_count = sum((degree + 1) * (degree + 2) // 2 for degree in DEGREES)
    table = np.zeros((filter_count, filter_count, term_count))
    counter = 0
    for family, degree in enumerate(DEGREES):
        for along_x in range(degree + 1):
            for along_y in range(degree + 1 - along_x):
                table[starts[family] + along_x, starts[family] + along_y, counter] = 1.0
                counter += 1
    return table


def band_tables(tile_side):
    filters = basis_filters()
    source = np.arange(tile_side)[:, None]
    target = np.arange(tile_side)[None, :]
    shift_table = target - source
    inside = np.abs(shift_table) <= REACH
    picked = filters[:, np.clip(shift_table + REACH, 0, 2 * REACH)] * inside
    row_table = np.transpose(picked, (1, 0, 2))
    column_table = np.transpose(picked, (0, 2, 1))
    row_half = jnp.asarray(row_table, jnp.float32).astype(jnp.bfloat16)
    column_half = jnp.asarray(column_table, jnp.float32).astype(jnp.bfloat16)
    return row_half, column_half, jnp.asarray(term_table(), jnp.float32)


def match_block(tile_block, coef_block):
    row_half, column_half, expand = band_tables(tile_block.shape[-1])
    rowpass = jnp.einsum('nyz,zfx->nyfx', tile_block.astype(jnp.float32), row_half.astype(jnp.float32),
                         precision=lax.Precision.HIGHEST)
    mixing = jnp.einsum('nt,fgt->nfg', coef_block.astype(jnp.float32), expand, precision=lax.Precision.HIGHEST)
    mixed_half = jnp.einsum('nyfx,nfg->nygx', rowpass, mixing, precision=lax.Precision.HIGHEST).astype(jnp.bfloat16)
    mixed_half = lax.optimization_barrier(mixed_half)
    return jnp.einsum('gyz,nzgx->nyx', column_half.astype(jnp.float32), mixed_half.astype(jnp.float32),
                      precision=lax.Precision.HIGHEST)


def tile_mask(pad_values, tile_side):
    pixel_line = jnp.arange(tile_side, dtype=jnp.float32)[None, :]
    rows_ok = (pixel_line >= pad_values[:, 0:1]) & (pixel_line < tile_side - pad_values[:, 1:2])
    cols_ok = (pixel_line >= pad_values[:, 2:3]) & (pixel_line < tile_side - pad_values[:, 3:4])
    return (rows_ok[:, :, None] & cols_ok[:, None, :]).astype(jnp.float32)


def reference(tile_flux, inverse_var, kernel_coef, owner_index, offsets, pad_widths):
    chi_total = jnp.zeros((PATCHES, PATCH_SIDE, PATCH_SIDE), jnp.float32)
    coadd_list = []
    for band_index in range(BANDS):
        blocks = tile_flux[band_index].reshape(-1, 8, TILE, TILE)
        coef_blocks = kernel_coef[band_index].reshape(-1, 8, TERMS)
        matched = lax.map(lambda pair: match_block(pair[0], pair[1]), (blocks, coef_blocks))
        matched = matched.reshape(-1, TILE, TILE)
        weight = inverse_var[band_index].astype(jnp.float32) * tile_mask(
            pad_widths[band_index].astype(jnp.float32), TILE)
        weighted = weight * matched
        band_owner = owner_index[band_index, :, 0].astype(jnp.int32)
        band_corner = (offsets[band_index] * 8).astype(jnp.int32)

        def place(tile_index, totals):
            flux_sum, weight_sum = totals
            corner = (band_owner[tile_index], band_corner[tile_index, 0], band_corner[tile_index, 1])
            region = lax.dynamic_slice(flux_sum, corner, (1, TILE, TILE)) + weighted[tile_index][None]
            flux_sum = lax.dynamic_update_slice(flux_sum, region, corner)
            region = lax.dynamic_slice(weight_sum, corner, (1, TILE, TILE)) + weight[tile_index][None]
            weight_sum = lax.dynamic_update_slice(weight_sum, region, corner)
            return flux_sum, weight_sum

        empty = jnp.zeros((PATCHES, PATCH_SIDE, PATCH_SIDE), jnp.float32)
        flux_sum, weight_sum = lax.fori_loop(0, EXPOSURE_TILES, place, (empty, empty))
        denominator = weight_sum + 1.0
        coadd_list.append(flux_sum / denominator)
        chi_total = chi_total + flux_sum * flux_sum / denominator
    return jnp.stack(coadd_list), chi_total
```

```python
import functools

import jax
import jax.numpy as jnp
import ml_dtypes
import numpy as np
from jax import lax
from jax.experimental import pallas as pl
from jax.experimental.pallas import tpu as pltpu
from jax.sharding import PartitionSpec as P

PATCH_SIDE = 512
TILE = 128
TILES_DEV = 8
PATCHES = 8
CAP = 2
SPREADS = (0.7, 1.5, 3.0)
DEGREES = (4, 2, 2)
REACH = 10
STARTS = (0, 5, 8)
FILTERS = 11
META_ROWS = 16
STRIP = 32
STRIPS = PATCH_SIDE // STRIP
COL_BLOCKS = PATCH_SIDE // TILE
F32 = jnp.float32
BF16 = jnp.bfloat16


def basis_filters():
    offsets_axis = np.arange(-REACH, REACH + 1) * 1.0
    filters = []
    for spread_value, degree in zip(SPREADS, DEGREES):
        profile = np.exp(-(offsets_axis**2) / (2.0 * spread_value * spread_value))
        profile = profile / profile.sum()
        for exponent in range(degree + 1):
            filters.append(profile * (offsets_axis / REACH) ** exponent)
    return np.stack(filters)


def band_tables():
    filters = basis_filters()
    source = np.arange(TILE)[:, None]
    target = np.arange(TILE)[None, :]
    shift_table = target - source
    inside = np.abs(shift_table) <= REACH
    picked = filters[:, np.clip(shift_table + REACH, 0, 2 * REACH)] * inside
    row_table = np.transpose(picked, (1, 0, 2)).reshape(TILE, FILTERS * TILE)
    column_table = np.transpose(picked, (2, 0, 1)).reshape(TILE, FILTERS * TILE)
    half = lambda table: table.astype(np.float32).astype(ml_dtypes.bfloat16)
    return half(row_table), half(column_table)


def term_list():
    terms = [[] for _ in range(FILTERS)]
    counter = 0
    for family, degree in enumerate(DEGREES):
        for along_x in range(degree + 1):
            for along_y in range(degree + 1 - along_x):
                terms[STARTS[family] + along_y].append((STARTS[family] + along_x, counter))
                counter += 1
    return terms


TERM_LIST = term_list()


def slot_of(owner_ref, tile):
    patch = owner_ref[tile, 0]
    rank = jnp.int32(0)
    for other in range(tile):
        rank = rank + jnp.where(owner_ref[other, 0] == patch, 1, 0).astype(jnp.int32)
    return patch, rank


def masked_weight(var_tile, pads_ref, tile):
    line_y = lax.broadcasted_iota(jnp.int32, (TILE, TILE), 0)
    line_x = lax.broadcasted_iota(jnp.int32, (TILE, TILE), 1)
    inside = (
        (line_y >= pads_ref[tile, 0])
        & (line_y < TILE - pads_ref[tile, 1])
        & (line_x >= pads_ref[tile, 2])
        & (line_x < TILE - pads_ref[tile, 3])
    )
    return jnp.where(inside, var_tile.astype(F32), 0.0)


def weight_kernel(owner_ref, offsets_ref, pads_ref, var_ref, out_ref):
    out_ref[...] = jnp.zeros_like(out_ref)
    line = lax.broadcasted_iota(jnp.int32, (META_ROWS, TILE), 0)
    for tile in range(TILES_DEV):
        patch, rank = slot_of(owner_ref, tile)
        start = pl.multiple_of(rank * TILE, TILE)
        out_ref[patch, pl.ds(start, TILE), :] = masked_weight(
            var_ref[tile], pads_ref, tile
        ).astype(BF16)
        row_offset = offsets_ref[tile, 0].astype(F32)
        col_offset = offsets_ref[tile, 1].astype(F32)
        place = line - rank * 4
        entry = jnp.where(
            place == 0, 1.0, jnp.where(place == 1, row_offset, jnp.where(place == 2, col_offset, 0.0))
        )
        meta = out_ref[patch, CAP * TILE :, :].astype(F32)
        out_ref[patch, CAP * TILE :, :] = (meta + entry).astype(BF16)


def match_kernel(
    owner_ref, pads_ref, coef_ref, flux_ref, var_ref, row_ref, col_ref, out_ref, rowpass, mixed
):
    out_ref[...] = jnp.zeros_like(out_ref)
    for first in range(0, TILES_DEV, 2):
        side = (first // 2) % 2
        pair = flux_ref[first : first + 2].reshape(2 * TILE, TILE)
        rowpass[side] = jnp.dot(pair, row_ref[...], preferred_element_type=F32)
        for part in range(2):
            tile = first + part
            coefs = [coef_ref[tile, k] for k in range(27)]
            for block in range(0, TILE, 16):
                rows = slice(part * TILE + block, part * TILE + block + 16)
                lines = [rowpass[side, rows, f * TILE : (f + 1) * TILE] for f in range(FILTERS)]
                for g in range(FILTERS):
                    total = None
                    for f, k in TERM_LIST[g]:
                        term = lines[f] * coefs[k]
                        total = term if total is None else total + term
                    mixed[side, g * TILE + block : g * TILE + block + 16,
                          part * TILE : (part + 1) * TILE] = total.astype(BF16)
        matched = jnp.dot(col_ref[...], mixed[side], preferred_element_type=F32)
        for part in range(2):
            tile = first + part
            patch, rank = slot_of(owner_ref, tile)
            start = pl.multiple_of(rank * TILE, TILE)
            weight = masked_weight(var_ref[tile], pads_ref, tile)
            out_ref[patch, pl.ds(start, TILE), :] = (
                weight * matched[:, part * TILE : (part + 1) * TILE]
            ).astype(BF16)


def scatter_kernel(meta_ref, tiles_ref, out_ref, image):
    image[...] = jnp.zeros_like(image)
    lane = lax.broadcasted_iota(jnp.int32, (TILE, TILE), 1)
    for source in range(PATCHES):
        for rank in range(CAP):

            @pl.when(meta_ref[source, rank * 4] != 0)
            def _():
                row = pl.multiple_of(meta_ref[source, rank * 4 + 1] * 8, 8)
                column = meta_ref[source, rank * 4 + 2] * 8
                block = column // TILE
                shift = column - block * TILE
                tile = tiles_ref[source, rank * TILE : (rank + 1) * TILE, :].astype(F32)
                turned = pltpu.roll(tile, shift, 1)
                image[block, pl.ds(row, TILE), :] += jnp.where(lane >= shift, turned, 0.0)
                image[block + 1, pl.ds(row, TILE), :] += jnp.where(lane < shift, turned, 0.0)

    for strip in range(STRIPS):
        for block in range(COL_BLOCKS):
            out_ref[strip, :, block * TILE : (block + 1) * TILE] = image[
                block, strip * STRIP : (strip + 1) * STRIP, :
            ].astype(BF16)


def reduce_kernel(flux_ref, weight_ref, coadd_ref, chi_ref):
    flux = flux_ref[0].astype(F32)
    weight = weight_ref[0].astype(F32)
    for strip in range(1, STRIPS):
        flux = flux + flux_ref[strip].astype(F32)
        weight = weight + weight_ref[strip].astype(F32)
    coadd = flux / (weight + 1.0)
    coadd_ref[...] = coadd
    chi = (flux * coadd).astype(BF16)
    for band in range(chi_ref.shape[0]):
        chi_ref[band] = chi


def chi_kernel(parts_ref, out_ref):
    total = parts_ref[0].astype(F32)
    for band in range(1, parts_ref.shape[0]):
        total = total + parts_ref[band].astype(F32)
    out_ref[...] = total


SMEM = pl.BlockSpec(memory_space=pltpu.SMEM)
VMEM = pl.BlockSpec(memory_space=pltpu.VMEM)
PARAMS = pltpu.CompilerParams(vmem_limit_bytes=32 * 1024 * 1024)


def scatter(meta, tiles):
    return pl.pallas_call(
        scatter_kernel,
        out_shape=jax.ShapeDtypeStruct((STRIPS, STRIP, PATCH_SIDE), BF16),
        in_specs=[SMEM, VMEM],
        out_specs=VMEM,
        scratch_shapes=[pltpu.VMEM((COL_BLOCKS + 1, PATCH_SIDE, TILE), F32)],
        compiler_params=PARAMS,
        cost_estimate=pl.CostEstimate(flops=10_000_000, bytes_accessed=2_000_000, transcendentals=0),
    )(meta, tiles)


def on_device(tile_flux, inverse_var, kernel_coef, owner_index, offsets, pad_widths):
    row_table, column_table = band_tables()
    owner, corner, pads = owner_index[0], offsets[0], pad_widths[0]
    bands = lax.axis_size("band")
    with jax.named_scope("weight_slots"):
        weight_slots = pl.pallas_call(
            weight_kernel,
            out_shape=jax.ShapeDtypeStruct((PATCHES, CAP * TILE + META_ROWS, TILE), BF16),
            in_specs=[SMEM, SMEM, SMEM, VMEM],
            out_specs=VMEM,
            compiler_params=PARAMS,
        )(owner, corner, pads, inverse_var[0])
    weight_got = lax.all_to_all(weight_slots, "patch", 0, 0, tiled=True)
    with jax.named_scope("flux_slots"):
        flux_slots = pl.pallas_call(
            match_kernel,
            out_shape=jax.ShapeDtypeStruct((PATCHES, CAP * TILE, TILE), BF16),
            in_specs=[SMEM, SMEM, SMEM, VMEM, VMEM, VMEM, VMEM],
            out_specs=VMEM,
            scratch_shapes=[
                pltpu.VMEM((2, 2 * TILE, FILTERS * TILE), F32),
                pltpu.VMEM((2, FILTERS * TILE, 2 * TILE), BF16),
            ],
            compiler_params=PARAMS,
            cost_estimate=pl.CostEstimate(
                flops=750_000_000, bytes_accessed=2_000_000, transcendentals=0
            ),
        )(
            owner,
            pads,
            kernel_coef[0].astype(F32),
            tile_flux[0],
            inverse_var[0],
            jnp.asarray(row_table),
            jnp.asarray(column_table),
        )
    flux_got = lax.all_to_all(flux_slots, "patch", 0, 0, tiled=True)
    meta = weight_got[:, CAP * TILE : CAP * TILE + 8, 0].astype(jnp.int32)
    with jax.named_scope("weight_image"):
        weight_image = scatter(meta, weight_got)
    weight_strips = lax.all_to_all(weight_image, "group", 0, 0, tiled=True)
    with jax.named_scope("flux_image"):
        flux_image = scatter(meta, flux_got)
    flux_strips = lax.all_to_all(flux_image, "group", 0, 0, tiled=True)
    with jax.named_scope("strip_sums"):
        coadd, chi_copies = pl.pallas_call(
            reduce_kernel,
            out_shape=(
                jax.ShapeDtypeStruct((STRIP, PATCH_SIDE), F32),
                jax.ShapeDtypeStruct((bands, STRIP, PATCH_SIDE), BF16),
            ),
            in_specs=[VMEM, VMEM],
            out_specs=(VMEM, VMEM),
            compiler_params=PARAMS,
        )(flux_strips, weight_strips)
    chi_parts = lax.all_to_all(chi_copies, "band", 0, 0, tiled=True)
    with jax.named_scope("chi_sum"):
        chi = pl.pallas_call(
            chi_kernel,
            out_shape=jax.ShapeDtypeStruct((STRIP, PATCH_SIDE), F32),
            in_specs=[VMEM],
            out_specs=VMEM,
            compiler_params=PARAMS,
        )(chi_parts)
    return (coadd[None, None], chi[None])


def solution(mesh):
    return jax.shard_map(
        on_device,
        mesh=mesh,
        in_specs=(
            P("band", ("group", "patch"), None, None),
            P("band", ("group", "patch"), None, None),
            P("band", ("group", "patch"), None),
            P("band", ("group", "patch"), None),
            P("band", ("group", "patch"), None),
            P("band", ("group", "patch"), None),
        ),
        out_specs=(P("band", "patch", "group", None), P("patch", "group", None)),
        check_vma=False,
    )
```

```python
import jax
import jax.numpy as jnp
import ml_dtypes
import numpy as np
from jax import lax
from jax.experimental import pallas as pl
from jax.experimental.pallas import tpu as pltpu
from jax.sharding import PartitionSpec as P

PATCH_SIDE = 512
TILE = 128
TILES_DEV = 8
PATCHES = 8
CAP = 2
SPREADS = (0.7, 1.5, 3.0)
DEGREES = (4, 2, 2)
REACH = 10
STARTS = (0, 5, 8)
FILTERS = 11
META_ROWS = 16
SLOT_ROWS = 2 * CAP * 64
STRIP = 32
STRIPS = PATCH_SIDE // STRIP
HALF = STRIPS // 2
COL_BLOCKS = PATCH_SIDE // TILE
F32 = jnp.float32
BF16 = jnp.bfloat16


def basis_filters():
    offsets_axis = np.arange(-REACH, REACH + 1) * 1.0
    filters = []
    for spread_value, degree in zip(SPREADS, DEGREES):
        profile = np.exp(-(offsets_axis**2) / (2.0 * spread_value * spread_value))
        profile = profile / profile.sum()
        for exponent in range(degree + 1):
            filters.append(profile * (offsets_axis / REACH) ** exponent)
    return np.stack(filters)


def band_tables():
    filters = basis_filters()
    source = np.arange(TILE)[:, None]
    target = np.arange(TILE)[None, :]
    shift_table = target - source
    inside = np.abs(shift_table) <= REACH
    picked = filters[:, np.clip(shift_table + REACH, 0, 2 * REACH)] * inside
    row_table = np.transpose(picked, (1, 0, 2)).reshape(TILE, FILTERS * TILE)
    column_table = np.transpose(picked, (2, 0, 1)).reshape(TILE, FILTERS * TILE)
    half = lambda table: table.astype(np.float32).astype(ml_dtypes.bfloat16)
    return half(row_table), half(column_table)


def term_list():
    terms = [[] for _ in range(FILTERS)]
    counter = 0
    for family, degree in enumerate(DEGREES):
        for along_x in range(degree + 1):
            for along_y in range(degree + 1 - along_x):
                terms[STARTS[family] + along_y].append((STARTS[family] + along_x, counter))
                counter += 1
    return terms


TERM_LIST = term_list()


def slot_of(owner_ref, offsets_ref, tile):
    patch = owner_ref[0, tile]
    rank = jnp.int32(0)
    before = [jnp.int32(0), jnp.int32(0)]
    for other in range(tile):
        same = owner_ref[0, other] == patch
        rank = rank + jnp.where(same, 1, 0)
        before = [v + jnp.where(same, offsets_ref[i, other], 0) for i, v in enumerate(before)]
    return patch, rank, before


def first_row(row_offset, parity):
    row = row_offset * 8
    return (row // 64) * STRIP + jnp.clip(row % 64 - STRIP * parity, 0, STRIP)


def masked_weight(var_tile, pads_ref, tile):
    line_y = lax.broadcasted_iota(jnp.int32, (TILE, TILE), 0)
    line_x = lax.broadcasted_iota(jnp.int32, (TILE, TILE), 1)
    inside = (
        (line_y >= pads_ref[0, tile])
        & (line_y < TILE - pads_ref[1, tile])
        & (line_x >= pads_ref[2, tile])
        & (line_x < TILE - pads_ref[3, tile])
    )
    return jnp.where(inside, var_tile.astype(F32), 0.0)


def slot_kernel(
    owner_ref, offsets_ref, pads_ref, coef_hbm, flux_hbm, var_hbm, row_hbm, col_hbm, out_ref,
    coef_half, coef_full, coef_ref, flux_ref, var_ref, row_ref, col_ref, rowpass, mixed, whole, sems,
):
    pairs = (
        (coef_hbm, coef_half),
        (row_hbm, row_ref),
        (flux_hbm, flux_ref),
        (col_hbm, col_ref),
        (var_hbm, var_ref),
    )
    copies = [pltpu.make_async_copy(a, b, sems.at[i]) for i, (a, b) in enumerate(pairs)]
    for copy in copies:
        copy.start()
    out_ref[...] = jnp.zeros_like(out_ref)
    line = lax.broadcasted_iota(jnp.int32, (META_ROWS, TILE), 0)
    slots = []
    for tile in range(TILES_DEV):
        patch, rank, before = slot_of(owner_ref, offsets_ref, tile)
        slots.append((patch, rank))
        now = [offsets_ref[0, tile], offsets_ref[1, tile]]
        second = rank > 0
        entry = [jnp.int32(1)] + [jnp.where(second, u, v) for u, v in zip(before, now)]
        entry = entry + [jnp.int32(0), rank] + [jnp.where(second, v, 0) for v in now]
        meta = jnp.zeros((META_ROWS, TILE), F32)
        for i, value in enumerate(entry):
            if i != 3:
                meta = jnp.where(line == i, value.astype(F32), meta)
        meta = meta.astype(BF16)
        for parity in range(2):
            out_ref[parity * PATCHES + patch, SLOT_ROWS:, :] = meta
    copies[0].wait()
    coef_full[...] = coef_half[...].astype(F32)
    spread = pltpu.make_async_copy(coef_full, coef_ref, sems.at[5])
    spread.start()
    copies[1].wait()
    copies[2].wait()
    for first in range(0, TILES_DEV, 2):
        side = (first // 2) % 2
        pair = flux_ref[first : first + 2].reshape(2 * TILE, TILE)
        rowpass[side] = jnp.dot(pair, row_ref[...], preferred_element_type=F32)
        for part in range(2):
            if first + part == 0:
                spread.wait()
            coefs = [coef_ref[first + part, k] for k in range(27)]
            for block in range(0, TILE, 16):
                rows = slice(part * TILE + block, part * TILE + block + 16)
                lines = [rowpass[side, rows, f * TILE : (f + 1) * TILE] for f in range(FILTERS)]
                for g in range(FILTERS):
                    total = None
                    for f, k in TERM_LIST[g]:
                        term = lines[f] * coefs[k]
                        total = term if total is None else total + term
                    mixed[side, g * TILE + block : g * TILE + block + 16,
                          part * TILE : (part + 1) * TILE] = total.astype(BF16)
        if first == 0:
            copies[3].wait()
            copies[4].wait()
        matched = jnp.dot(col_ref[...], mixed[side], preferred_element_type=F32)
        for part in range(2):
            tile = first + part
            patch, rank = slots[tile]
            weight = masked_weight(var_ref[tile], pads_ref, tile)
            whole[side, part, 0] = weight * matched[:, part * TILE : (part + 1) * TILE]
            whole[side, part, 1] = weight
            for parity in range(2):
                top = first_row(offsets_ref[0, tile], parity)
                taken = []
                for group in range(8):
                    at = top + 8 * group
                    row = (at // STRIP) * 64 + STRIP * parity + at % STRIP - offsets_ref[0, tile] * 8
                    taken.append(pl.multiple_of(row, 8))
                for image in range(2):
                    start = pl.multiple_of(image * CAP * 64 + rank * 64, 64)
                    rows = [whole[side, part, image, pl.ds(row, 8), :] for row in taken]
                    out_ref[parity * PATCHES + patch, pl.ds(start, 64), :] = jnp.concatenate(
                        rows, axis=0
                    ).astype(BF16)


def scatter_kernel(meta_ref, slots_ref, out_ref, images):
    images[...] = jnp.zeros_like(images)
    parity = lax.rem(lax.axis_index("group"), 2)
    lane = lax.broadcasted_iota(jnp.int32, (64, TILE), 1)
    for source in range(2 * PATCHES):
        for rank in range(CAP):

            @pl.when(meta_ref[source, rank * 4] != 0)
            def _():
                row = pl.multiple_of(first_row(meta_ref[source, rank * 4 + 1], parity), 8)
                column = meta_ref[source, rank * 4 + 2] * 8
                block = column // TILE
                shift = column % TILE
                for image in range(2):
                    start = image * CAP * 64 + rank * 64
                    half = slots_ref[source, start : start + 64, :].astype(F32)
                    turned = pltpu.roll(half, shift, 1)
                    place = (image, block, pl.ds(row, 64), slice(None))
                    images[place] += jnp.where(lane >= shift, turned, 0.0)
                    place = (image, block + 1, pl.ds(row, 64), slice(None))
                    images[place] += jnp.where(lane < shift, turned, 0.0)

    for half in range(HALF):
        for image in range(2):
            for block in range(COL_BLOCKS):
                out_ref[half, image, :, block * TILE : (block + 1) * TILE] = images[
                    image, block, half * STRIP : (half + 1) * STRIP, :
                ].astype(BF16)


def reduce_kernel(strips_ref, coadd_ref, chi_ref):
    flux = strips_ref[0, 0].astype(F32)
    weight = strips_ref[0, 1].astype(F32)
    for half in range(1, HALF):
        flux = flux + strips_ref[half, 0].astype(F32)
        weight = weight + strips_ref[half, 1].astype(F32)
    coadd = flux / (weight + 1.0)
    coadd_ref[...] = coadd
    chi = (flux * coadd).astype(BF16)
    for band in range(chi_ref.shape[0]):
        chi_ref[band] = chi


def chi_kernel(parts_ref, out_ref):
    total = parts_ref[0].astype(F32)
    for band in range(1, parts_ref.shape[0]):
        total = total + parts_ref[band].astype(F32)
    out_ref[...] = total


SMEM = pl.BlockSpec(memory_space=pltpu.SMEM)
VMEM = pl.BlockSpec(memory_space=pltpu.VMEM)
HBM = pl.BlockSpec(memory_space=pltpu.HBM)
VMEM_ALL = 60 * 1024 * 1024
PARAMS = pltpu.CompilerParams(vmem_limit_bytes=32 * 1024 * 1024)


def on_device(tile_flux, inverse_var, kernel_coef, owner_index, offsets, pad_widths):
    row_table, column_table = band_tables()
    owner, corner, pads = owner_index[0].T, offsets[0].T, pad_widths[0].T
    bands = lax.axis_size("band")
    with jax.named_scope("tile_slots"):
        slots = pl.pallas_call(
            slot_kernel,
            out_shape=jax.ShapeDtypeStruct((2 * PATCHES, SLOT_ROWS + META_ROWS, TILE), BF16),
            in_specs=[SMEM] * 3 + [HBM] * 5,
            out_specs=VMEM,
            scratch_shapes=[
                pltpu.VMEM((TILES_DEV, 27), BF16),
                pltpu.VMEM((TILES_DEV, 27), F32),
                pltpu.SMEM((TILES_DEV, 27), F32),
                pltpu.VMEM((TILES_DEV, TILE, TILE), BF16),
                pltpu.VMEM((TILES_DEV, TILE, TILE), BF16),
                pltpu.VMEM((TILE, FILTERS * TILE), BF16),
                pltpu.VMEM((TILE, FILTERS * TILE), BF16),
                pltpu.VMEM((2, 2 * TILE, FILTERS * TILE), F32),
                pltpu.VMEM((2, FILTERS * TILE, 2 * TILE), BF16),
                pltpu.VMEM((2, 2, 2, TILE, TILE), F32),
                pltpu.SemaphoreType.DMA((6,)),
            ],
            compiler_params=pltpu.CompilerParams(vmem_limit_bytes=VMEM_ALL),
        )(
            owner,
            corner,
            pads,
            kernel_coef[0],
            tile_flux[0],
            inverse_var[0],
            jnp.asarray(row_table),
            jnp.asarray(column_table),
        )
    blocks = [
        [z * PATCHES + patch for z in (low, low + 1) for patch in range(PATCHES)]
        for low in range(0, STRIPS, 2)
    ]
    slots_got = lax.all_to_all(
        slots, ("group", "patch"), 0, 0, tiled=True, axis_index_groups=blocks
    )
    meta = slots_got[:, SLOT_ROWS : SLOT_ROWS + 8, 0].astype(jnp.int32)
    with jax.named_scope("strip_images"):
        strips = pl.pallas_call(
            scatter_kernel,
            out_shape=jax.ShapeDtypeStruct((HALF, 2, STRIP, PATCH_SIDE), BF16),
            in_specs=[SMEM, VMEM],
            out_specs=VMEM,
            scratch_shapes=[pltpu.VMEM((2, COL_BLOCKS + 1, PATCH_SIDE // 2, TILE), F32)],
            compiler_params=PARAMS,
        )(meta, slots_got)
    parities = [list(range(parity, STRIPS, 2)) for parity in range(2)]
    strips_got = lax.all_to_all(strips, "group", 0, 0, tiled=True, axis_index_groups=parities)
    with jax.named_scope("strip_sums"):
        coadd, chi_copies = pl.pallas_call(
            reduce_kernel,
            out_shape=(
                jax.ShapeDtypeStruct((STRIP, PATCH_SIDE), F32),
                jax.ShapeDtypeStruct((bands, STRIP, PATCH_SIDE), BF16),
            ),
            in_specs=[VMEM],
            out_specs=(VMEM, VMEM),
            compiler_params=PARAMS,
        )(strips_got)
    chi_parts = lax.all_to_all(chi_copies, "band", 0, 0, tiled=True)
    with jax.named_scope("chi_sum"):
        chi = pl.pallas_call(
            chi_kernel,
            out_shape=jax.ShapeDtypeStruct((STRIP, PATCH_SIDE), F32),
            in_specs=[VMEM],
            out_specs=VMEM,
            compiler_params=PARAMS,
        )(chi_parts)
    return (coadd[None, None], chi[None])


def solution(mesh):
    return jax.shard_map(
        on_device,
        mesh=mesh,
        in_specs=(
            P("band", ("group", "patch"), None, None),
            P("band", ("group", "patch"), None, None),
            P("band", ("group", "patch"), None),
            P("band", ("group", "patch"), None),
            P("band", ("group", "patch"), None),
            P("band", ("group", "patch"), None),
        ),
        out_specs=(P("band", "patch", "group", None), P("patch", "group", None)),
        check_vma=False,
    )
```

```python
import jax
import jax.numpy as jnp
import ml_dtypes
import numpy as np
from jax import lax
from jax.experimental import pallas as pl
from jax.experimental.pallas import tpu as pltpu
from jax.sharding import PartitionSpec as P

PATCH_SIDE = 512
TILE = 128
TILES_DEV = 8
PATCHES = 8
CAP = 2
SPREADS = (0.7, 1.5, 3.0)
DEGREES = (4, 2, 2)
REACH = 10
STARTS = (0, 5, 8)
FILTERS = 11
META_ROWS = 16
SLOT_ROWS = 2 * CAP * 64
STRIP = 32
STRIPS = PATCH_SIDE // STRIP
HALF = STRIPS // 2
COL_BLOCKS = PATCH_SIDE // TILE
F32 = jnp.float32
BF16 = jnp.bfloat16


def basis_filters():
    offsets_axis = np.arange(-REACH, REACH + 1) * 1.0
    filters = []
    for spread_value, degree in zip(SPREADS, DEGREES):
        profile = np.exp(-(offsets_axis**2) / (2.0 * spread_value * spread_value))
        profile = profile / profile.sum()
        for exponent in range(degree + 1):
            filters.append(profile * (offsets_axis / REACH) ** exponent)
    return np.stack(filters)


def band_tables():
    filters = basis_filters()
    source = np.arange(TILE)[:, None]
    target = np.arange(TILE)[None, :]
    shift_table = target - source
    inside = np.abs(shift_table) <= REACH
    picked = filters[:, np.clip(shift_table + REACH, 0, 2 * REACH)] * inside
    row_table = np.transpose(picked, (1, 0, 2)).reshape(TILE, FILTERS * TILE)
    column_table = np.transpose(picked, (2, 0, 1)).reshape(TILE, FILTERS * TILE)
    half = lambda table: table.astype(np.float32).astype(ml_dtypes.bfloat16)
    return half(row_table), half(column_table)


def term_list():
    terms = [[] for _ in range(FILTERS)]
    counter = 0
    for family, degree in enumerate(DEGREES):
        for along_x in range(degree + 1):
            for along_y in range(degree + 1 - along_x):
                terms[STARTS[family] + along_y].append((STARTS[family] + along_x, counter))
                counter += 1
    return terms


TERM_LIST = term_list()


def slot_of(owner_ref, offsets_ref, tile):
    patch = owner_ref[0, tile]
    rank = jnp.int32(0)
    before = [jnp.int32(0), jnp.int32(0)]
    for other in range(tile):
        same = owner_ref[0, other] == patch
        rank = rank + jnp.where(same, 1, 0)
        before = [v + jnp.where(same, offsets_ref[i, other], 0) for i, v in enumerate(before)]
    return patch, rank, before


def first_row(row_offset, parity):
    row = row_offset * 8
    return (row // 64) * STRIP + jnp.clip(row % 64 - STRIP * parity, 0, STRIP)


def masked_weight(var_tile, pads_ref, tile):
    line_y = lax.broadcasted_iota(jnp.int32, (TILE, TILE), 0)
    line_x = lax.broadcasted_iota(jnp.int32, (TILE, TILE), 1)
    inside = (
        (line_y >= pads_ref[0, tile])
        & (line_y < TILE - pads_ref[1, tile])
        & (line_x >= pads_ref[2, tile])
        & (line_x < TILE - pads_ref[3, tile])
    )
    return jnp.where(inside, var_tile.astype(F32), 0.0)


def slot_kernel(
    owner_hbm, offsets_hbm, pads_hbm, coef_hbm, flux_hbm, var_hbm, row_hbm, col_hbm, out_hbm,
    owner_ref, offsets_ref, pads_ref, coef_half, coef_full, coef_ref, flux_ref, var_ref, row_ref,
    col_ref, rowpass, mixed, whole, halves, metas, sems, out_sems,
):
    pairs = (
        (owner_hbm, owner_ref),
        (offsets_hbm, offsets_ref),
        (coef_hbm, coef_half),
        (row_hbm, row_ref),
        (flux_hbm, flux_ref),
        (pads_hbm, pads_ref),
        (col_hbm, col_ref),
        (var_hbm, var_ref),
    )
    copies = [pltpu.make_async_copy(a, b, sems.at[i]) for i, (a, b) in enumerate(pairs)]
    for copy in copies:
        copy.start()
    metas[...] = jnp.zeros_like(metas)
    line = lax.broadcasted_iota(jnp.int32, (META_ROWS, TILE), 0)
    for copy in copies[:3]:
        copy.wait()
    coef_full[...] = coef_half[...].astype(F32)
    spread = pltpu.make_async_copy(coef_full, coef_ref, sems.at[len(pairs)])
    spread.start()
    slots = []
    for tile in range(TILES_DEV):
        patch, rank, before = slot_of(owner_ref, offsets_ref, tile)
        slots.append((patch, rank))
        now = [offsets_ref[0, tile], offsets_ref[1, tile]]
        second = rank > 0
        entry = [jnp.int32(1)] + [jnp.where(second, u, v) for u, v in zip(before, now)]
        entry = entry + [jnp.int32(0), rank] + [jnp.where(second, v, 0) for v in now]
        meta = jnp.zeros((META_ROWS, TILE), F32)
        for i, value in enumerate(entry):
            if i != 3:
                meta = jnp.where(line == i, value.astype(F32), meta)
        meta = meta.astype(BF16)
        for parity in range(2):
            metas[parity * PATCHES + patch] = meta
    sent = [
        pltpu.make_async_copy(metas, out_hbm.at[:, pl.ds(SLOT_ROWS, META_ROWS), :], out_sems.at[0])
    ]
    sent[0].start()
    copies[3].wait()
    copies[4].wait()
    def row_pass(pair):
        tiles = flux_ref[2 * pair : 2 * pair + 2].reshape(2 * TILE, TILE)
        rowpass[pair % 2] = jnp.dot(tiles, row_ref[...], preferred_element_type=F32)

    def mix(pair):
        side = pair % 2
        for part in range(2):
            coefs = [coef_ref[2 * pair + part, k] for k in range(27)]
            for block in range(0, TILE, 16):
                rows = slice(part * TILE + block, part * TILE + block + 16)
                lines = [rowpass[side, rows, f * TILE : (f + 1) * TILE] for f in range(FILTERS)]
                for g in range(FILTERS):
                    total = None
                    for f, k in TERM_LIST[g]:
                        term = lines[f] * coefs[k]
                        total = term if total is None else total + term
                    mixed[side, g * TILE + block : g * TILE + block + 16,
                          part * TILE : (part + 1) * TILE] = total.astype(BF16)

    def column_pass(pair):
        return jnp.dot(col_ref[...], mixed[pair % 2], preferred_element_type=F32)

    def finish(pair, matched):
        for part in range(2):
            tile = 2 * pair + part
            patch, rank = slots[tile]
            weight = masked_weight(var_ref[tile], pads_ref, tile)
            whole[tile, 0] = weight * matched[:, part * TILE : (part + 1) * TILE]
            whole[tile, 1] = weight
            for parity in range(2):
                top = first_row(offsets_ref[0, tile], parity)
                taken = []
                for group in range(8):
                    at = top + 8 * group
                    row = (at // STRIP) * 64 + STRIP * parity + at % STRIP - offsets_ref[0, tile] * 8
                    taken.append(pl.multiple_of(row, 8))
                for image in range(2):
                    rows = [whole[tile, image, pl.ds(row, 8), :] for row in taken]
                    halves[tile, parity, image * 64 : (image + 1) * 64, :] = jnp.concatenate(
                        rows, axis=0
                    ).astype(BF16)
                start = pl.multiple_of(rank * TILE, TILE)
                copy = pltpu.make_async_copy(
                    halves.at[tile, parity],
                    out_hbm.at[parity * PATCHES + patch, pl.ds(start, TILE), :],
                    out_sems.at[1 + 2 * tile + parity],
                )
                copy.start()
                sent.append(copy)

    row_pass(0)
    spread.wait()
    for copy in copies[5:]:
        copy.wait()
    matched = None
    for pair in range(TILES_DEV // 2):
        if pair + 1 < TILES_DEV // 2:
            row_pass(pair + 1)
        mix(pair)
        if pair > 0:
            finish(pair - 1, matched)
        matched = column_pass(pair)
    finish(TILES_DEV // 2 - 1, matched)
    for copy in sent:
        copy.wait()


def scatter_kernel(meta_ref, slots_ref, out_ref, images):
    images[...] = jnp.zeros_like(images)
    parity = lax.rem(lax.axis_index("group"), 2)
    lane = lax.broadcasted_iota(jnp.int32, (64, TILE), 1)
    for rank in range(CAP):
        for source in range(2 * PATCHES):
            filled = meta_ref[source, rank * 4] != 0
            row = first_row(meta_ref[source, rank * 4 + 1], parity)
            row = pl.multiple_of(row, 8)
            column = meta_ref[source, rank * 4 + 2] * 8
            block = column // TILE
            shift = column % TILE
            right = lane >= jnp.where(filled, shift, TILE)
            left = lane < jnp.where(filled, shift, 0)
            for image in range(2):
                start = rank * TILE + image * 64
                half = slots_ref[source, start : start + 64, :].astype(F32)
                turned = pltpu.roll(half, shift, 1)
                place = (image, block, pl.ds(row, 64), slice(None))
                images[place] += jnp.where(right, turned, 0.0)
                place = (image, block + 1, pl.ds(row, 64), slice(None))
                images[place] += jnp.where(left, turned, 0.0)

    for half in range(HALF):
        for image in range(2):
            for block in range(COL_BLOCKS):
                out_ref[half, image, :, block * TILE : (block + 1) * TILE] = images[
                    image, block, half * STRIP : (half + 1) * STRIP, :
                ].astype(BF16)


def reduce_kernel(strips_ref, coadd_ref, chi_ref):
    flux = strips_ref[0, 0].astype(F32)
    weight = strips_ref[0, 1].astype(F32)
    for half in range(1, HALF):
        flux = flux + strips_ref[half, 0].astype(F32)
        weight = weight + strips_ref[half, 1].astype(F32)
    coadd = flux / (weight + 1.0)
    coadd_ref[...] = coadd
    chi = (flux * coadd).astype(BF16)
    for band in range(chi_ref.shape[0]):
        chi_ref[band] = chi


def chi_kernel(parts_ref, out_ref):
    total = parts_ref[0].astype(F32)
    for band in range(1, parts_ref.shape[0]):
        total = total + parts_ref[band].astype(F32)
    out_ref[...] = total


SMEM = pl.BlockSpec(memory_space=pltpu.SMEM)
VMEM = pl.BlockSpec(memory_space=pltpu.VMEM)
HBM = pl.BlockSpec(memory_space=pltpu.HBM)
VMEM_ALL = 60 * 1024 * 1024
PARAMS = pltpu.CompilerParams(vmem_limit_bytes=32 * 1024 * 1024)


def on_device(tile_flux, inverse_var, kernel_coef, owner_index, offsets, pad_widths):
    row_table, column_table = band_tables()
    owner, corner, pads = owner_index[0].T, offsets[0].T, pad_widths[0].T
    bands = lax.axis_size("band")
    with jax.named_scope("tile_slots"):
        slots = pl.pallas_call(
            slot_kernel,
            out_shape=jax.ShapeDtypeStruct((2 * PATCHES, SLOT_ROWS + META_ROWS, TILE), BF16),
            in_specs=[HBM] * 8,
            out_specs=HBM,
            scratch_shapes=[
                pltpu.SMEM((1, TILES_DEV), jnp.int32),
                pltpu.SMEM((2, TILES_DEV), jnp.int32),
                pltpu.SMEM((4, TILES_DEV), jnp.int32),
                pltpu.VMEM((TILES_DEV, 27), BF16),
                pltpu.VMEM((TILES_DEV, 27), F32),
                pltpu.SMEM((TILES_DEV, 27), F32),
                pltpu.VMEM((TILES_DEV, TILE, TILE), BF16),
                pltpu.VMEM((TILES_DEV, TILE, TILE), BF16),
                pltpu.VMEM((TILE, FILTERS * TILE), BF16),
                pltpu.VMEM((TILE, FILTERS * TILE), BF16),
                pltpu.VMEM((2, 2 * TILE, FILTERS * TILE), F32),
                pltpu.VMEM((2, FILTERS * TILE, 2 * TILE), BF16),
                pltpu.VMEM((TILES_DEV, 2, TILE, TILE), F32),
                pltpu.VMEM((TILES_DEV, 2, TILE, TILE), BF16),
                pltpu.VMEM((2 * PATCHES, META_ROWS, TILE), BF16),
                pltpu.SemaphoreType.DMA((9,)),
                pltpu.SemaphoreType.DMA((1 + 2 * TILES_DEV,)),
            ],
            compiler_params=pltpu.CompilerParams(vmem_limit_bytes=VMEM_ALL),
        )(
            owner,
            corner,
            pads,
            kernel_coef[0],
            tile_flux[0],
            inverse_var[0],
            jnp.asarray(row_table),
            jnp.asarray(column_table),
        )
    blocks = [
        [z * PATCHES + patch for z in (low, low + 1) for patch in range(PATCHES)]
        for low in range(0, STRIPS, 2)
    ]
    slots_got = lax.all_to_all(
        slots, ("group", "patch"), 0, 0, tiled=True, axis_index_groups=blocks
    )
    meta = slots_got[:, SLOT_ROWS : SLOT_ROWS + 8, 0].astype(jnp.int32)
    with jax.named_scope("strip_images"):
        strips = pl.pallas_call(
            scatter_kernel,
            out_shape=jax.ShapeDtypeStruct((HALF, 2, STRIP, PATCH_SIDE), BF16),
            in_specs=[SMEM, VMEM],
            out_specs=VMEM,
            scratch_shapes=[pltpu.VMEM((2, COL_BLOCKS + 1, PATCH_SIDE // 2, TILE), F32)],
            compiler_params=PARAMS,
        )(meta, slots_got)
    parities = [list(range(parity, STRIPS, 2)) for parity in range(2)]
    strips_got = lax.all_to_all(strips, "group", 0, 0, tiled=True, axis_index_groups=parities)
    with jax.named_scope("strip_sums"):
        coadd, chi_copies = pl.pallas_call(
            reduce_kernel,
            out_shape=(
                jax.ShapeDtypeStruct((STRIP, PATCH_SIDE), F32),
                jax.ShapeDtypeStruct((bands, STRIP, PATCH_SIDE), BF16),
            ),
            in_specs=[VMEM],
            out_specs=(VMEM, VMEM),
            compiler_params=PARAMS,
        )(strips_got)
    chi_parts = lax.all_to_all(chi_copies, "band", 0, 0, tiled=True)
    with jax.named_scope("chi_sum"):
        chi = pl.pallas_call(
            chi_kernel,
            out_shape=jax.ShapeDtypeStruct((STRIP, PATCH_SIDE), F32),
            in_specs=[VMEM],
            out_specs=VMEM,
            compiler_params=PARAMS,
        )(chi_parts)
    return (coadd[None, None], chi[None])


def solution(mesh):
    return jax.shard_map(
        on_device,
        mesh=mesh,
        in_specs=(
            P("band", ("group", "patch"), None, None),
            P("band", ("group", "patch"), None, None),
            P("band", ("group", "patch"), None),
            P("band", ("group", "patch"), None),
            P("band", ("group", "patch"), None),
            P("band", ("group", "patch"), None),
        ),
        out_specs=(P("band", "patch", "group", None), P("patch", "group", None)),
        check_vma=False,
    )
```

```python
import jax
import jax.numpy as jnp
import ml_dtypes
import numpy as np
from jax import lax
from jax.experimental import pallas as pl
from jax.experimental.pallas import tpu as pltpu
from jax.sharding import PartitionSpec as P

PATCH_SIDE = 512
TILE = 128
TILES_DEV = 8
PATCHES = 8
CAP = 2
SPREADS = (0.7, 1.5, 3.0)
DEGREES = (4, 2, 2)
REACH = 10
STARTS = (0, 5, 8)
FILTERS = 11
META_ROWS = 16
SLOT_ROWS = 2 * CAP * 64
STRIP = 32
STRIPS = PATCH_SIDE // STRIP
HALF = STRIPS // 2
COL_BLOCKS = PATCH_SIDE // TILE
F32 = jnp.float32
BF16 = jnp.bfloat16


def basis_filters():
    offsets_axis = np.arange(-REACH, REACH + 1) * 1.0
    filters = []
    for spread_value, degree in zip(SPREADS, DEGREES):
        profile = np.exp(-(offsets_axis**2) / (2.0 * spread_value * spread_value))
        profile = profile / profile.sum()
        for exponent in range(degree + 1):
            filters.append(profile * (offsets_axis / REACH) ** exponent)
    return np.stack(filters)


def band_tables():
    filters = basis_filters()
    source = np.arange(TILE)[:, None]
    target = np.arange(TILE)[None, :]
    shift_table = target - source
    inside = np.abs(shift_table) <= REACH
    picked = filters[:, np.clip(shift_table + REACH, 0, 2 * REACH)] * inside
    row_table = np.transpose(picked, (1, 0, 2)).reshape(TILE, FILTERS * TILE)
    column_table = np.transpose(picked, (2, 0, 1)).reshape(TILE, FILTERS * TILE)
    half = lambda table: table.astype(np.float32).astype(ml_dtypes.bfloat16)
    return half(row_table), half(column_table)


def term_list():
    terms = [[] for _ in range(FILTERS)]
    counter = 0
    for family, degree in enumerate(DEGREES):
        for along_x in range(degree + 1):
            for along_y in range(degree + 1 - along_x):
                terms[STARTS[family] + along_y].append((STARTS[family] + along_x, counter))
                counter += 1
    return terms


TERM_LIST = term_list()


def slots_of(owner_ref, offsets_ref):
    patches = [owner_ref[0, tile] for tile in range(TILES_DEV)]
    codes = [(1 << 16) + (offsets_ref[0, t] << 8) + offsets_ref[1, t] for t in range(TILES_DEV)]
    slots = []
    for tile in range(TILES_DEV):
        seen = jnp.int32(0)
        for other in range(tile):
            seen = seen + jnp.where(patches[other] == patches[tile], codes[other], 0)
        slots.append((patches[tile], seen >> 16, (seen >> 8) & 255, seen & 255))
    return slots


def first_row(row_offset, parity):
    row = row_offset * 8
    return (row >> 6) * STRIP + jnp.clip((row & 63) - STRIP * parity, 0, STRIP)


def rows_of_parity(row_offset, parity):
    ahead = (4 * parity - row_offset) & 7
    cut = jnp.where(ahead > 4, 8 - ahead, 0)
    start = jnp.where(ahead > 4, 0, ahead * 8)
    return [pl.multiple_of(start + 8 * i + (((cut + i) >> 2) << 5), 8) for i in range(4)]


def masked_weight(var_tile, pads_ref, tile):
    line_y = lax.broadcasted_iota(jnp.int32, (TILE, TILE), 0)
    line_x = lax.broadcasted_iota(jnp.int32, (TILE, TILE), 1)
    inside = (
        (line_y >= pads_ref[0, tile])
        & (line_y < TILE - pads_ref[1, tile])
        & (line_x >= pads_ref[2, tile])
        & (line_x < TILE - pads_ref[3, tile])
    )
    return jnp.where(inside, var_tile.astype(F32), 0.0)


def slot_kernel(
    owner_hbm, offsets_hbm, pads_hbm, coef_hbm, flux_hbm, var_hbm, row_hbm, col_hbm, out_hbm,
    owner_ref, offsets_ref, pads_ref, coef_half, coef_full, coef_ref, flux_ref, var_ref, row_ref,
    col_ref, rowpass, mixed, whole, halves, metas, sems, out_sems,
):
    pairs = (
        (owner_hbm, owner_ref),
        (offsets_hbm, offsets_ref),
        (coef_hbm, coef_half),
        (row_hbm, row_ref),
        (flux_hbm, flux_ref),
        (pads_hbm, pads_ref),
        (col_hbm, col_ref),
        (var_hbm, var_ref),
    )
    copies = [pltpu.make_async_copy(a, b, sems.at[i]) for i, (a, b) in enumerate(pairs)]
    for copy in copies:
        copy.start()
    metas[...] = jnp.zeros_like(metas)
    line = lax.broadcasted_iota(jnp.int32, (META_ROWS, TILE), 0)
    for copy in copies[:3]:
        copy.wait()
    coef_full[...] = coef_half[...].astype(F32)
    spread = pltpu.make_async_copy(coef_full, coef_ref, sems.at[len(pairs)])
    spread.start()
    slots = slots_of(owner_ref, offsets_ref)
    for tile in range(TILES_DEV):
        patch, rank, row_before, col_before = slots[tile]
        row_now, col_now = offsets_ref[0, tile], offsets_ref[1, tile]
        second = rank > 0
        entry = {
            0: jnp.int32(1),
            1: jnp.where(second, row_before, row_now),
            2: jnp.where(second, col_before, col_now),
            4: rank,
            5: jnp.where(second, row_now, 0),
            6: jnp.where(second, col_now, 0),
        }
        meta = jnp.zeros((META_ROWS, TILE), jnp.int32)
        for i, value in entry.items():
            meta = jnp.where(line == i, value, meta)
        meta = meta.astype(F32).astype(BF16)
        for parity in range(2):
            metas[parity, patch] = meta
    sent = [
        pltpu.make_async_copy(metas, out_hbm.at[:, :, pl.ds(SLOT_ROWS, META_ROWS), :], out_sems.at[0])
    ]
    sent[0].start()
    copies[3].wait()
    copies[4].wait()
    def row_pass(pair):
        tiles = flux_ref[2 * pair : 2 * pair + 2].reshape(2 * TILE, TILE)
        rowpass[pair % 2] = jnp.dot(tiles, row_ref[...], preferred_element_type=F32)

    def mix(pair):
        side = pair % 2
        for part in range(2):
            coefs = [coef_ref[2 * pair + part, k] for k in range(27)]
            for block in range(0, TILE, 16):
                rows = slice(part * TILE + block, part * TILE + block + 16)
                lines = [rowpass[side, rows, f * TILE : (f + 1) * TILE] for f in range(FILTERS)]
                for g in range(FILTERS):
                    total = None
                    for f, k in TERM_LIST[g]:
                        term = lines[f] * coefs[k]
                        total = term if total is None else total + term
                    mixed[side, g * TILE + block : g * TILE + block + 16,
                          part * TILE : (part + 1) * TILE] = total.astype(BF16)

    def column_pass(pair):
        return jnp.dot(col_ref[...], mixed[pair % 2], preferred_element_type=F32)

    def finish(pair, matched):
        for part in range(2):
            tile = 2 * pair + part
            patch, rank = slots[tile][:2]
            weight = masked_weight(var_ref[tile], pads_ref, tile)
            whole[tile, 0] = weight * matched[:, part * TILE : (part + 1) * TILE]
            whole[tile, 1] = weight
            for parity in range(2):
                taken = rows_of_parity(offsets_ref[0, tile], parity)
                taken = taken + [pl.multiple_of(row + 64, 8) for row in taken]
                for image in range(2):
                    rows = [whole[tile, image, pl.ds(row, 8), :] for row in taken]
                    halves[tile, parity, image * 64 : (image + 1) * 64, :] = jnp.concatenate(
                        rows, axis=0
                    ).astype(BF16)
            start = pl.multiple_of(rank * TILE, TILE)
            copy = pltpu.make_async_copy(
                halves.at[tile],
                out_hbm.at[:, patch, pl.ds(start, TILE), :],
                out_sems.at[1 + tile],
            )
            copy.start()
            sent.append(copy)

    row_pass(0)
    spread.wait()
    for copy in copies[5:]:
        copy.wait()
    matched = None
    for pair in range(TILES_DEV // 2):
        if pair + 1 < TILES_DEV // 2:
            row_pass(pair + 1)
        mix(pair)
        if pair > 0:
            finish(pair - 1, matched)
        matched = column_pass(pair)
    finish(TILES_DEV // 2 - 1, matched)
    for copy in sent:
        copy.wait()


def scatter_kernel(meta_ref, slots_ref, out_ref, images):
    images[...] = jnp.zeros_like(images)
    parity = lax.rem(lax.axis_index("group"), 2)
    lane = lax.broadcasted_iota(jnp.int32, (64, TILE), 1)
    for rank in range(CAP):
        for source in range(2 * PATCHES):
            filled = meta_ref[source, rank * 4] != 0
            row = first_row(meta_ref[source, rank * 4 + 1], parity)
            row = pl.multiple_of(row, 8)
            column = meta_ref[source, rank * 4 + 2] * 8
            block = column >> 7
            shift = column & (TILE - 1)
            right = lane >= jnp.where(filled, shift, TILE)
            left = lane < jnp.where(filled, shift, 0)
            for image in range(2):
                start = rank * TILE + image * 64
                half = slots_ref[source, start : start + 64, :].astype(F32)
                turned = pltpu.roll(half, shift, 1)
                place = (image, block, pl.ds(row, 64), slice(None))
                images[place] += jnp.where(right, turned, 0.0)
                place = (image, block + 1, pl.ds(row, 64), slice(None))
                images[place] += jnp.where(left, turned, 0.0)

    for half in range(HALF):
        for image in range(2):
            for block in range(COL_BLOCKS):
                out_ref[half, image, :, block * TILE : (block + 1) * TILE] = images[
                    image, block, half * STRIP : (half + 1) * STRIP, :
                ].astype(BF16)


def reduce_kernel(strips_ref, coadd_ref, chi_ref):
    flux = strips_ref[0, 0].astype(F32)
    weight = strips_ref[0, 1].astype(F32)
    for half in range(1, HALF):
        flux = flux + strips_ref[half, 0].astype(F32)
        weight = weight + strips_ref[half, 1].astype(F32)
    coadd = flux / (weight + 1.0)
    coadd_ref[...] = coadd
    chi = (flux * coadd).astype(BF16)
    for band in range(chi_ref.shape[0]):
        chi_ref[band] = chi


def chi_kernel(parts_ref, out_ref):
    total = parts_ref[0].astype(F32)
    for band in range(1, parts_ref.shape[0]):
        total = total + parts_ref[band].astype(F32)
    out_ref[...] = total


SMEM = pl.BlockSpec(memory_space=pltpu.SMEM)
VMEM = pl.BlockSpec(memory_space=pltpu.VMEM)
HBM = pl.BlockSpec(memory_space=pltpu.HBM)
VMEM_ALL = 60 * 1024 * 1024
PARAMS = pltpu.CompilerParams(vmem_limit_bytes=32 * 1024 * 1024)


def on_device(tile_flux, inverse_var, kernel_coef, owner_index, offsets, pad_widths):
    row_table, column_table = band_tables()
    owner, corner, pads = owner_index[0].T, offsets[0].T, pad_widths[0].T
    bands = lax.axis_size("band")
    with jax.named_scope("tile_slots"):
        slots = pl.pallas_call(
            slot_kernel,
            out_shape=jax.ShapeDtypeStruct((2, PATCHES, SLOT_ROWS + META_ROWS, TILE), BF16),
            in_specs=[HBM] * 8,
            out_specs=HBM,
            scratch_shapes=[
                pltpu.SMEM((1, TILES_DEV), jnp.int32),
                pltpu.SMEM((2, TILES_DEV), jnp.int32),
                pltpu.SMEM((4, TILES_DEV), jnp.int32),
                pltpu.VMEM((TILES_DEV, 27), BF16),
                pltpu.VMEM((TILES_DEV, 27), F32),
                pltpu.SMEM((TILES_DEV, 27), F32),
                pltpu.VMEM((TILES_DEV, TILE, TILE), BF16),
                pltpu.VMEM((TILES_DEV, TILE, TILE), BF16),
                pltpu.VMEM((TILE, FILTERS * TILE), BF16),
                pltpu.VMEM((TILE, FILTERS * TILE), BF16),
                pltpu.VMEM((2, 2 * TILE, FILTERS * TILE), F32),
                pltpu.VMEM((2, FILTERS * TILE, 2 * TILE), BF16),
                pltpu.VMEM((TILES_DEV, 2, TILE, TILE), F32),
                pltpu.VMEM((TILES_DEV, 2, TILE, TILE), BF16),
                pltpu.VMEM((2, PATCHES, META_ROWS, TILE), BF16),
                pltpu.SemaphoreType.DMA((9,)),
                pltpu.SemaphoreType.DMA((1 + TILES_DEV,)),
            ],
            compiler_params=pltpu.CompilerParams(vmem_limit_bytes=VMEM_ALL),
        )(
            owner,
            corner,
            pads,
            kernel_coef[0],
            tile_flux[0],
            inverse_var[0],
            jnp.asarray(row_table),
            jnp.asarray(column_table),
        )
    slots = slots.reshape((2 * PATCHES,) + slots.shape[2:])
    blocks = [
        [z * PATCHES + patch for z in (low, low + 1) for patch in range(PATCHES)]
        for low in range(0, STRIPS, 2)
    ]
    slots_got = lax.all_to_all(
        slots, ("group", "patch"), 0, 0, tiled=True, axis_index_groups=blocks
    )
    meta = slots_got[:, SLOT_ROWS : SLOT_ROWS + 8, 0].astype(jnp.int32)
    with jax.named_scope("strip_images"):
        strips = pl.pallas_call(
            scatter_kernel,
            out_shape=jax.ShapeDtypeStruct((HALF, 2, STRIP, PATCH_SIDE), BF16),
            in_specs=[SMEM, VMEM],
            out_specs=VMEM,
            scratch_shapes=[pltpu.VMEM((2, COL_BLOCKS + 1, PATCH_SIDE // 2, TILE), F32)],
            compiler_params=PARAMS,
        )(meta, slots_got)
    parities = [list(range(parity, STRIPS, 2)) for parity in range(2)]
    strips_got = lax.all_to_all(strips, "group", 0, 0, tiled=True, axis_index_groups=parities)
    with jax.named_scope("strip_sums"):
        coadd, chi_copies = pl.pallas_call(
            reduce_kernel,
            out_shape=(
                jax.ShapeDtypeStruct((STRIP, PATCH_SIDE), F32),
                jax.ShapeDtypeStruct((bands, STRIP, PATCH_SIDE), BF16),
            ),
            in_specs=[VMEM],
            out_specs=(VMEM, VMEM),
            compiler_params=PARAMS,
        )(strips_got)
    chi_parts = lax.all_to_all(chi_copies, "band", 0, 0, tiled=True)
    with jax.named_scope("chi_sum"):
        chi = pl.pallas_call(
            chi_kernel,
            out_shape=jax.ShapeDtypeStruct((STRIP, PATCH_SIDE), F32),
            in_specs=[VMEM],
            out_specs=VMEM,
            compiler_params=PARAMS,
        )(chi_parts)
    return (coadd[None, None], chi[None])


def solution(mesh):
    return jax.shard_map(
        on_device,
        mesh=mesh,
        in_specs=(
            P("band", ("group", "patch"), None, None),
            P("band", ("group", "patch"), None, None),
            P("band", ("group", "patch"), None),
            P("band", ("group", "patch"), None),
            P("band", ("group", "patch"), None),
            P("band", ("group", "patch"), None),
        ),
        out_specs=(P("band", "patch", "group", None), P("patch", "group", None)),
        check_vma=False,
    )
```

```python
import jax
import jax.numpy as jnp
import ml_dtypes
import numpy as np
from jax import lax
from jax.experimental import pallas as pl
from jax.experimental.pallas import tpu as pltpu
from jax.sharding import PartitionSpec as P

PATCH_SIDE = 512
TILE = 128
TILES_DEV = 8
PATCHES = 8
CAP = 2
SPREADS = (0.7, 1.5, 3.0)
DEGREES = (4, 2, 2)
REACH = 10
STARTS = (0, 5, 8)
FILTERS = 11
META_ROWS = 16
SLOT_ROWS = 2 * CAP * 64
STRIP = 32
STRIPS = PATCH_SIDE // STRIP
QUARTER = STRIPS // 4
COL_BLOCKS = PATCH_SIDE // TILE
F32 = jnp.float32
BF16 = jnp.bfloat16


def basis_filters():
    offsets_axis = np.arange(-REACH, REACH + 1) * 1.0
    filters = []
    for spread_value, degree in zip(SPREADS, DEGREES):
        profile = np.exp(-(offsets_axis**2) / (2.0 * spread_value * spread_value))
        profile = profile / profile.sum()
        for exponent in range(degree + 1):
            filters.append(profile * (offsets_axis / REACH) ** exponent)
    return np.stack(filters)


def band_tables():
    filters = basis_filters()
    source = np.arange(TILE)[:, None]
    target = np.arange(TILE)[None, :]
    shift_table = target - source
    inside = np.abs(shift_table) <= REACH
    picked = filters[:, np.clip(shift_table + REACH, 0, 2 * REACH)] * inside
    row_table = np.transpose(picked, (1, 0, 2)).reshape(TILE, FILTERS * TILE)
    column_table = np.transpose(picked, (2, 0, 1)).reshape(TILE, FILTERS * TILE)
    half = lambda table: table.astype(np.float32).astype(ml_dtypes.bfloat16)
    return half(row_table), half(column_table)


def term_list():
    terms = [[] for _ in range(FILTERS)]
    counter = 0
    for family, degree in enumerate(DEGREES):
        for along_x in range(degree + 1):
            for along_y in range(degree + 1 - along_x):
                terms[STARTS[family] + along_y].append((STARTS[family] + along_x, counter))
                counter += 1
    return terms


TERM_LIST = term_list()


def slots_of(owner_ref, offsets_ref):
    patches = [owner_ref[0, tile] for tile in range(TILES_DEV)]
    codes = [(1 << 16) + (offsets_ref[0, t] << 8) + offsets_ref[1, t] for t in range(TILES_DEV)]
    slots = []
    for tile in range(TILES_DEV):
        seen = jnp.int32(0)
        for other in range(tile):
            seen = seen + jnp.where(patches[other] == patches[tile], codes[other], 0)
        slots.append((patches[tile], seen >> 16, (seen >> 8) & 255, seen & 255))
    return slots


def first_row(row_offset, parity):
    row = row_offset * 8
    return (row >> 6) * STRIP + jnp.clip((row & 63) - STRIP * parity, 0, STRIP)


def rows_of_parity(row_offset, parity):
    ahead = (4 * parity - row_offset) & 7
    cut = jnp.where(ahead > 4, 8 - ahead, 0)
    start = jnp.where(ahead > 4, 0, ahead * 8)
    return [pl.multiple_of(start + 8 * i + (((cut + i) >> 2) << 5), 8) for i in range(4)]


def masked_weight(var_tile, pads_ref, tile):
    line_y = lax.broadcasted_iota(jnp.int32, (TILE, TILE), 0)
    line_x = lax.broadcasted_iota(jnp.int32, (TILE, TILE), 1)
    inside = (
        (line_y >= pads_ref[0, tile])
        & (line_y < TILE - pads_ref[1, tile])
        & (line_x >= pads_ref[2, tile])
        & (line_x < TILE - pads_ref[3, tile])
    )
    return jnp.where(inside, var_tile.astype(F32), 0.0)


def slot_kernel(
    owner_hbm, offsets_hbm, pads_hbm, coef_hbm, flux_hbm, var_hbm, row_hbm, col_hbm, out_hbm,
    owner_ref, offsets_ref, pads_ref, coef_half, coef_full, coef_ref, flux_ref, var_ref, row_ref,
    col_ref, rowpass, mixed, whole, halves, metas, sems, out_sems,
):
    pairs = (
        (owner_hbm, owner_ref),
        (offsets_hbm, offsets_ref),
        (coef_hbm, coef_half),
        (row_hbm, row_ref),
        (flux_hbm, flux_ref),
        (pads_hbm, pads_ref),
        (col_hbm, col_ref),
        (var_hbm, var_ref),
    )
    copies = [pltpu.make_async_copy(a, b, sems.at[i]) for i, (a, b) in enumerate(pairs)]
    for copy in copies:
        copy.start()
    metas[...] = jnp.zeros_like(metas)
    line = lax.broadcasted_iota(jnp.int32, (META_ROWS, TILE), 0)
    for copy in copies[:3]:
        copy.wait()
    coef_full[...] = coef_half[...].astype(F32)
    spread = pltpu.make_async_copy(coef_full, coef_ref, sems.at[len(pairs)])
    spread.start()
    slots = slots_of(owner_ref, offsets_ref)
    for tile in range(TILES_DEV):
        patch, rank, row_before, col_before = slots[tile]
        row_now, col_now = offsets_ref[0, tile], offsets_ref[1, tile]
        second = rank > 0
        entry = {
            0: jnp.int32(1),
            1: jnp.where(second, row_before, row_now),
            2: jnp.where(second, col_before, col_now),
            4: rank,
            5: jnp.where(second, row_now, 0),
            6: jnp.where(second, col_now, 0),
        }
        meta = jnp.zeros((META_ROWS, TILE), jnp.int32)
        for i, value in entry.items():
            meta = jnp.where(line == i, value, meta)
        meta = meta.astype(F32).astype(BF16)
        for parity in range(2):
            metas[parity, patch] = meta
    sent = [
        pltpu.make_async_copy(metas, out_hbm.at[:, :, pl.ds(SLOT_ROWS, META_ROWS), :], out_sems.at[0])
    ]
    sent[0].start()
    copies[3].wait()
    copies[4].wait()
    def row_pass(pair):
        tiles = flux_ref[2 * pair : 2 * pair + 2].reshape(2 * TILE, TILE)
        rowpass[pair % 2] = jnp.dot(tiles, row_ref[...], preferred_element_type=F32)

    def mix(pair):
        side = pair % 2
        for part in range(2):
            coefs = [coef_ref[2 * pair + part, k] for k in range(27)]
            for block in range(0, TILE, 16):
                rows = slice(part * TILE + block, part * TILE + block + 16)
                lines = [rowpass[side, rows, f * TILE : (f + 1) * TILE] for f in range(FILTERS)]
                for g in range(FILTERS):
                    total = None
                    for f, k in TERM_LIST[g]:
                        term = lines[f] * coefs[k]
                        total = term if total is None else total + term
                    mixed[side, g * TILE + block : g * TILE + block + 16,
                          part * TILE : (part + 1) * TILE] = total.astype(BF16)

    def column_pass(pair):
        return jnp.dot(col_ref[...], mixed[pair % 2], preferred_element_type=F32)

    def finish(pair, matched):
        for part in range(2):
            tile = 2 * pair + part
            patch, rank = slots[tile][:2]
            weight = masked_weight(var_ref[tile], pads_ref, tile)
            whole[tile, 0] = weight * matched[:, part * TILE : (part + 1) * TILE]
            whole[tile, 1] = weight
            for parity in range(2):
                taken = rows_of_parity(offsets_ref[0, tile], parity)
                taken = taken + [pl.multiple_of(row + 64, 8) for row in taken]
                for image in range(2):
                    rows = [whole[tile, image, pl.ds(row, 8), :] for row in taken]
                    halves[tile, parity, image * 64 : (image + 1) * 64, :] = jnp.concatenate(
                        rows, axis=0
                    ).astype(BF16)
            start = pl.multiple_of(rank * TILE, TILE)
            copy = pltpu.make_async_copy(
                halves.at[tile],
                out_hbm.at[:, patch, pl.ds(start, TILE), :],
                out_sems.at[1 + tile],
            )
            copy.start()
            sent.append(copy)

    row_pass(0)
    spread.wait()
    for copy in copies[5:]:
        copy.wait()
    matched = None
    for pair in range(TILES_DEV // 2):
        if pair + 1 < TILES_DEV // 2:
            row_pass(pair + 1)
        mix(pair)
        if pair > 0:
            finish(pair - 1, matched)
        matched = column_pass(pair)
    finish(TILES_DEV // 2 - 1, matched)
    for copy in sent:
        copy.wait()


def scatter_kernel(meta_ref, slots_ref, keep_ref, send_ref, images):
    images[...] = jnp.zeros_like(images)
    parity = lax.rem(lax.axis_index("group"), 2)
    lane = lax.broadcasted_iota(jnp.int32, (64, TILE), 1)
    for rank in range(CAP):
        for source in range(2 * PATCHES):
            filled = meta_ref[source, rank * 4] != 0
            row = first_row(meta_ref[source, rank * 4 + 1], parity)
            row = pl.multiple_of(row, 8)
            column = meta_ref[source, rank * 4 + 2] * 8
            block = column >> 7
            shift = column & (TILE - 1)
            right = lane >= jnp.where(filled, shift, TILE)
            left = lane < jnp.where(filled, shift, 0)
            for image in range(2):
                start = rank * TILE + image * 64
                half = slots_ref[source, start : start + 64, :].astype(F32)
                turned = pltpu.roll(half, shift, 1)
                place = (image, block, pl.ds(row, 64), slice(None))
                images[place] += jnp.where(right, turned, 0.0)
                place = (image, block + 1, pl.ds(row, 64), slice(None))
                images[place] += jnp.where(left, turned, 0.0)

    own = (lax.axis_index("group") >> 1) & 1
    for entry in range(QUARTER):
        kept = pl.multiple_of((2 * entry + own) * STRIP, STRIP)
        sent = pl.multiple_of((2 * entry + 1 - own) * STRIP, STRIP)
        for image in range(2):
            for block in range(COL_BLOCKS):
                columns = slice(block * TILE, (block + 1) * TILE)
                keep_ref[entry, image, :, columns] = images[image, block, pl.ds(kept, STRIP), :]
                send_ref[entry, image, :, columns] = images[
                    image, block, pl.ds(sent, STRIP), :
                ].astype(BF16)


def quad_kernel(keep_ref, got_ref, own_ref, *out_refs):
    here = lax.axis_index("group") >> 2
    own_ref[...] = keep_ref[here] + got_ref[here].astype(F32)
    for step, out_ref in enumerate(out_refs, 1):
        entry = (here + step) & (QUARTER - 1)
        out_ref[...] = (keep_ref[entry] + got_ref[entry].astype(F32)).astype(BF16)


def reduce_kernel(own_ref, *refs):
    strip_refs, (coadd_ref, chi_ref) = refs[:-2], refs[-2:]
    flux, weight = own_ref[0], own_ref[1]
    for strip_ref in strip_refs:
        flux = flux + strip_ref[0].astype(F32)
        weight = weight + strip_ref[1].astype(F32)
    coadd = flux / (weight + 1.0)
    coadd_ref[...] = coadd
    chi = (flux * coadd).astype(BF16)
    for band in range(chi_ref.shape[0]):
        chi_ref[band] = chi


def chi_kernel(parts_ref, out_ref):
    total = parts_ref[0].astype(F32)
    for band in range(1, parts_ref.shape[0]):
        total = total + parts_ref[band].astype(F32)
    out_ref[...] = total


SMEM = pl.BlockSpec(memory_space=pltpu.SMEM)
VMEM = pl.BlockSpec(memory_space=pltpu.VMEM)
HBM = pl.BlockSpec(memory_space=pltpu.HBM)
VMEM_ALL = 60 * 1024 * 1024
PARAMS = pltpu.CompilerParams(vmem_limit_bytes=32 * 1024 * 1024)


def on_device(tile_flux, inverse_var, kernel_coef, owner_index, offsets, pad_widths):
    row_table, column_table = band_tables()
    owner, corner, pads = owner_index[0].T, offsets[0].T, pad_widths[0].T
    bands = lax.axis_size("band")
    with jax.named_scope("tile_slots"):
        slots = pl.pallas_call(
            slot_kernel,
            out_shape=jax.ShapeDtypeStruct((2, PATCHES, SLOT_ROWS + META_ROWS, TILE), BF16),
            in_specs=[HBM] * 8,
            out_specs=HBM,
            scratch_shapes=[
                pltpu.SMEM((1, TILES_DEV), jnp.int32),
                pltpu.SMEM((2, TILES_DEV), jnp.int32),
                pltpu.SMEM((4, TILES_DEV), jnp.int32),
                pltpu.VMEM((TILES_DEV, 27), BF16),
                pltpu.VMEM((TILES_DEV, 27), F32),
                pltpu.SMEM((TILES_DEV, 27), F32),
                pltpu.VMEM((TILES_DEV, TILE, TILE), BF16),
                pltpu.VMEM((TILES_DEV, TILE, TILE), BF16),
                pltpu.VMEM((TILE, FILTERS * TILE), BF16),
                pltpu.VMEM((TILE, FILTERS * TILE), BF16),
                pltpu.VMEM((2, 2 * TILE, FILTERS * TILE), F32),
                pltpu.VMEM((2, FILTERS * TILE, 2 * TILE), BF16),
                pltpu.VMEM((TILES_DEV, 2, TILE, TILE), F32),
                pltpu.VMEM((TILES_DEV, 2, TILE, TILE), BF16),
                pltpu.VMEM((2, PATCHES, META_ROWS, TILE), BF16),
                pltpu.SemaphoreType.DMA((9,)),
                pltpu.SemaphoreType.DMA((1 + TILES_DEV,)),
            ],
            compiler_params=pltpu.CompilerParams(vmem_limit_bytes=VMEM_ALL),
        )(
            owner,
            corner,
            pads,
            kernel_coef[0],
            tile_flux[0],
            inverse_var[0],
            jnp.asarray(row_table),
            jnp.asarray(column_table),
        )
    slots = slots.reshape((2 * PATCHES,) + slots.shape[2:])
    blocks = [
        [z * PATCHES + patch for z in (low, low + 1) for patch in range(PATCHES)]
        for low in range(0, STRIPS, 2)
    ]
    slots_got = lax.all_to_all(
        slots, ("group", "patch"), 0, 0, tiled=True, axis_index_groups=blocks
    )
    meta = slots_got[:, SLOT_ROWS : SLOT_ROWS + 8, 0].astype(jnp.int32)
    with jax.named_scope("strip_images"):
        kept, sent = pl.pallas_call(
            scatter_kernel,
            out_shape=(
                jax.ShapeDtypeStruct((QUARTER, 2, STRIP, PATCH_SIDE), F32),
                jax.ShapeDtypeStruct((QUARTER, 2, STRIP, PATCH_SIDE), BF16),
            ),
            in_specs=[SMEM, VMEM],
            out_specs=(VMEM, VMEM),
            scratch_shapes=[pltpu.VMEM((2, COL_BLOCKS + 1, PATCH_SIDE // 2, TILE), F32)],
            compiler_params=PARAMS,
        )(meta, slots_got)
    pairs = []
    for z in range(STRIPS):
        for patch in range(PATCHES):
            shift = 2 if (z >> 1) % 2 == patch % 2 else -2
            pairs.append((z * PATCHES + patch, (z + shift) % STRIPS * PATCHES + patch))
    got = lax.ppermute(sent, ("group", "patch"), pairs)
    with jax.named_scope("quad_sums"):
        quads = pl.pallas_call(
            quad_kernel,
            out_shape=(jax.ShapeDtypeStruct((2, STRIP, PATCH_SIDE), F32),)
            + (jax.ShapeDtypeStruct((2, STRIP, PATCH_SIDE), BF16),) * (QUARTER - 1),
            in_specs=[VMEM, VMEM],
            out_specs=(VMEM,) * QUARTER,
            compiler_params=PARAMS,
        )(kept, got)
    strips_got = [quads[0]]
    for step in (2,1,3):
        ring = [(z, (z + 4 * step) % STRIPS) for z in range(STRIPS)]
        strips_got.append(lax.ppermute(quads[step], "group", ring))
    with jax.named_scope("strip_sums"):
        coadd, chi_copies = pl.pallas_call(
            reduce_kernel,
            out_shape=(
                jax.ShapeDtypeStruct((STRIP, PATCH_SIDE), F32),
                jax.ShapeDtypeStruct((bands, STRIP, PATCH_SIDE), BF16),
            ),
            in_specs=[VMEM] * QUARTER,
            out_specs=(VMEM, VMEM),
            compiler_params=PARAMS,
        )(*strips_got)
    chi_parts = lax.all_to_all(chi_copies, "band", 0, 0, tiled=True)
    with jax.named_scope("chi_sum"):
        chi = pl.pallas_call(
            chi_kernel,
            out_shape=jax.ShapeDtypeStruct((STRIP, PATCH_SIDE), F32),
            in_specs=[VMEM],
            out_specs=VMEM,
            compiler_params=PARAMS,
        )(chi_parts)
    return (coadd[None, None], chi[None])


def solution(mesh):
    return jax.shard_map(
        on_device,
        mesh=mesh,
        in_specs=(
            P("band", ("group", "patch"), None, None),
            P("band", ("group", "patch"), None, None),
            P("band", ("group", "patch"), None),
            P("band", ("group", "patch"), None),
            P("band", ("group", "patch"), None),
            P("band", ("group", "patch"), None),
        ),
        out_specs=(P("band", "patch", "group", None), P("patch", "group", None)),
        check_vma=False,
    )
```

```python
import jax
import jax.numpy as jnp
import ml_dtypes
import numpy as np
from jax import lax
from jax.experimental import pallas as pl
from jax.experimental.pallas import tpu as pltpu
from jax.sharding import PartitionSpec as P

PATCH_SIDE = 512
TILE = 128
TILES_DEV = 8
PATCHES = 8
CAP = 2
SPREADS = (0.7, 1.5, 3.0)
DEGREES = (4, 2, 2)
REACH = 10
STARTS = (0, 5, 8)
FILTERS = 11
META_ROWS = 16
SLOT_ROWS = 2 * CAP * 64
STRIP = 32
STRIPS = PATCH_SIDE // STRIP
QUARTER = STRIPS // 4
COL_BLOCKS = PATCH_SIDE // TILE
F32 = jnp.float32
BF16 = jnp.bfloat16


def basis_filters():
    offsets_axis = np.arange(-REACH, REACH + 1) * 1.0
    filters = []
    for spread_value, degree in zip(SPREADS, DEGREES):
        profile = np.exp(-(offsets_axis**2) / (2.0 * spread_value * spread_value))
        profile = profile / profile.sum()
        for exponent in range(degree + 1):
            filters.append(profile * (offsets_axis / REACH) ** exponent)
    return np.stack(filters)


def band_tables():
    filters = basis_filters()
    source = np.arange(TILE)[:, None]
    target = np.arange(TILE)[None, :]
    shift_table = target - source
    inside = np.abs(shift_table) <= REACH
    picked = filters[:, np.clip(shift_table + REACH, 0, 2 * REACH)] * inside
    row_table = np.transpose(picked, (1, 0, 2)).reshape(TILE, FILTERS * TILE)
    column_table = np.transpose(picked, (2, 0, 1)).reshape(TILE, FILTERS * TILE)
    half = lambda table: table.astype(np.float32).astype(ml_dtypes.bfloat16)
    return half(row_table), half(column_table)


def term_list():
    terms = [[] for _ in range(FILTERS)]
    counter = 0
    for family, degree in enumerate(DEGREES):
        for along_x in range(degree + 1):
            for along_y in range(degree + 1 - along_x):
                terms[STARTS[family] + along_y].append((STARTS[family] + along_x, counter))
                counter += 1
    return terms


TERM_LIST = term_list()


def slots_of(owner_ref, offsets_ref):
    patches = [owner_ref[0, tile] for tile in range(TILES_DEV)]
    codes = [(1 << 16) + (offsets_ref[0, t] << 8) + offsets_ref[1, t] for t in range(TILES_DEV)]
    slots = []
    for tile in range(TILES_DEV):
        seen = jnp.int32(0)
        for other in range(tile):
            seen = seen + jnp.where(patches[other] == patches[tile], codes[other], 0)
        slots.append((patches[tile], seen >> 16, (seen >> 8) & 255, seen & 255))
    return slots


def first_row(row_offset, parity):
    row = row_offset * 8
    return (row >> 6) * STRIP + jnp.clip((row & 63) - STRIP * parity, 0, STRIP)


def rows_of_parity(row_offset, parity):
    ahead = (4 * parity - row_offset) & 7
    cut = jnp.where(ahead > 4, 8 - ahead, 0)
    start = jnp.where(ahead > 4, 0, ahead * 8)
    return [pl.multiple_of(start + 8 * i + (((cut + i) >> 2) << 5), 8) for i in range(4)]


def masked_weight(var_tile, pads_ref, tile):
    line_y = lax.broadcasted_iota(jnp.int32, (TILE, TILE), 0)
    line_x = lax.broadcasted_iota(jnp.int32, (TILE, TILE), 1)
    inside = (
        (line_y >= pads_ref[0, tile])
        & (line_y < TILE - pads_ref[1, tile])
        & (line_x >= pads_ref[2, tile])
        & (line_x < TILE - pads_ref[3, tile])
    )
    return jnp.where(inside, var_tile.astype(F32), 0.0)


def slot_kernel(
    owner_hbm, offsets_hbm, pads_hbm, coef_hbm, flux_hbm, var_hbm, row_hbm, col_hbm, out_hbm,
    owner_ref, offsets_ref, pads_ref, coef_half, coef_full, coef_ref, flux_ref, var_ref, row_ref,
    col_ref, rowpass, mixed, whole, halves, metas, sems, out_sems,
):
    pairs = (
        (owner_hbm, owner_ref),
        (offsets_hbm, offsets_ref),
        (coef_hbm, coef_half),
        (row_hbm, row_ref),
        (flux_hbm, flux_ref),
        (pads_hbm, pads_ref),
        (col_hbm, col_ref),
        (var_hbm, var_ref),
    )
    copies = [pltpu.make_async_copy(a, b, sems.at[i]) for i, (a, b) in enumerate(pairs)]
    for copy in copies:
        copy.start()
    metas[...] = jnp.zeros_like(metas)
    line = lax.broadcasted_iota(jnp.int32, (META_ROWS, TILE), 0)
    for copy in copies[:3]:
        copy.wait()
    coef_full[...] = coef_half[...].astype(F32)
    spread = pltpu.make_async_copy(coef_full, coef_ref, sems.at[len(pairs)])
    spread.start()
    slots = slots_of(owner_ref, offsets_ref)
    for tile in range(TILES_DEV):
        patch, rank, row_before, col_before = slots[tile]
        row_now, col_now = offsets_ref[0, tile], offsets_ref[1, tile]
        second = rank > 0
        entry = {
            0: jnp.int32(1),
            1: jnp.where(second, row_before, row_now),
            2: jnp.where(second, col_before, col_now),
            4: rank,
            5: jnp.where(second, row_now, 0),
            6: jnp.where(second, col_now, 0),
        }
        meta = jnp.zeros((META_ROWS, TILE), jnp.int32)
        for i, value in entry.items():
            meta = jnp.where(line == i, value, meta)
        meta = meta.astype(F32).astype(BF16)
        for parity in range(2):
            metas[parity, patch] = meta
    sent = [
        pltpu.make_async_copy(metas, out_hbm.at[:, :, pl.ds(SLOT_ROWS, META_ROWS), :], out_sems.at[0])
    ]
    sent[0].start()
    copies[3].wait()
    copies[4].wait()
    def row_pass(pair):
        tiles = flux_ref[2 * pair : 2 * pair + 2].reshape(2 * TILE, TILE)
        rowpass[pair % 2] = jnp.dot(tiles, row_ref[...], preferred_element_type=F32)

    def mix(pair):
        side = pair % 2
        for part in range(2):
            coefs = [coef_ref[2 * pair + part, k] for k in range(27)]
            for block in range(0, TILE, 16):
                rows = slice(part * TILE + block, part * TILE + block + 16)
                lines = [rowpass[side, rows, f * TILE : (f + 1) * TILE] for f in range(FILTERS)]
                for g in range(FILTERS):
                    total = None
                    for f, k in TERM_LIST[g]:
                        term = lines[f] * coefs[k]
                        total = term if total is None else total + term
                    mixed[side, g * TILE + block : g * TILE + block + 16,
                          part * TILE : (part + 1) * TILE] = total.astype(BF16)

    def column_pass(pair):
        return jnp.dot(col_ref[...], mixed[pair % 2], preferred_element_type=F32)

    def finish(pair, matched):
        for part in range(2):
            tile = 2 * pair + part
            patch, rank = slots[tile][:2]
            weight = masked_weight(var_ref[tile], pads_ref, tile)
            whole[tile, 0] = weight * matched[:, part * TILE : (part + 1) * TILE]
            whole[tile, 1] = weight
            for parity in range(2):
                taken = rows_of_parity(offsets_ref[0, tile], parity)
                taken = taken + [pl.multiple_of(row + 64, 8) for row in taken]
                for image in range(2):
                    rows = [whole[tile, image, pl.ds(row, 8), :] for row in taken]
                    halves[tile, parity, image * 64 : (image + 1) * 64, :] = jnp.concatenate(
                        rows, axis=0
                    ).astype(BF16)
            start = pl.multiple_of(rank * TILE, TILE)
            copy = pltpu.make_async_copy(
                halves.at[tile],
                out_hbm.at[:, patch, pl.ds(start, TILE), :],
                out_sems.at[1 + tile],
            )
            copy.start()
            sent.append(copy)

    row_pass(0)
    spread.wait()
    for copy in copies[5:]:
        copy.wait()
    matched = None
    for pair in range(TILES_DEV // 2):
        if pair + 1 < TILES_DEV // 2:
            row_pass(pair + 1)
        mix(pair)
        if pair > 0:
            finish(pair - 1, matched)
        matched = column_pass(pair)
    finish(TILES_DEV // 2 - 1, matched)
    for copy in sent:
        copy.wait()


def scatter_kernel(meta_ref, slots_ref, keep_ref, send_ref, images):
    images[...] = jnp.zeros_like(images)
    parity = lax.rem(lax.axis_index("group"), 2)
    lane = lax.broadcasted_iota(jnp.int32, (64, TILE), 1)
    for rank in range(CAP):
        for source in range(2 * PATCHES):
            filled = meta_ref[source, rank * 4] != 0
            row = first_row(meta_ref[source, rank * 4 + 1], parity)
            row = pl.multiple_of(row, 8)
            column = meta_ref[source, rank * 4 + 2] * 8
            block = column >> 7
            shift = column & (TILE - 1)
            right = lane >= jnp.where(filled, shift, TILE)
            left = lane < jnp.where(filled, shift, 0)
            for image in range(2):
                start = rank * TILE + image * 64
                half = slots_ref[source, start : start + 64, :].astype(F32)
                turned = pltpu.roll(half, shift, 1)
                place = (image, block, pl.ds(row, 64), slice(None))
                images[place] += jnp.where(right, turned, 0.0)
                place = (image, block + 1, pl.ds(row, 64), slice(None))
                images[place] += jnp.where(left, turned, 0.0)

    own = (lax.axis_index("group") >> 1) & 1
    for entry in range(QUARTER):
        kept = pl.multiple_of((2 * entry + own) * STRIP, STRIP)
        sent = pl.multiple_of((2 * entry + 1 - own) * STRIP, STRIP)
        for image in range(2):
            for block in range(COL_BLOCKS):
                columns = slice(block * TILE, (block + 1) * TILE)
                keep_ref[entry, image, :, columns] = images[image, block, pl.ds(kept, STRIP), :]
                send_ref[entry, image, :, columns] = images[
                    image, block, pl.ds(sent, STRIP), :
                ].astype(BF16)


def quad_kernel(keep_ref, got_ref, own_ref, *out_refs):
    here = lax.axis_index("group") >> 2
    own_ref[...] = keep_ref[here] + got_ref[here].astype(F32)
    for step, out_ref in enumerate(out_refs, 1):
        entry = (here + step) & (QUARTER - 1)
        out_ref[...] = (keep_ref[entry] + got_ref[entry].astype(F32)).astype(BF16)


def reduce_kernel(own_ref, *refs):
    strip_refs, (coadd_ref, chi_ref) = refs[:-2], refs[-2:]
    flux, weight = own_ref[0], own_ref[1]
    for strip_ref in strip_refs:
        flux = flux + strip_ref[0].astype(F32)
        weight = weight + strip_ref[1].astype(F32)
    coadd = flux / (weight + 1.0)
    coadd_ref[...] = coadd
    chi = (flux * coadd).astype(BF16)
    for band in range(chi_ref.shape[0]):
        chi_ref[band] = chi


def chi_kernel(coadd_ref, parts_ref, coadd_out, chi_out):
    coadd_out[...] = coadd_ref[...]
    total = parts_ref[0].astype(F32)
    for band in range(1, parts_ref.shape[0]):
        total = total + parts_ref[band].astype(F32)
    chi_out[...] = total


SMEM = pl.BlockSpec(memory_space=pltpu.SMEM)
VMEM = pl.BlockSpec(memory_space=pltpu.VMEM)
HBM = pl.BlockSpec(memory_space=pltpu.HBM)
VMEM_ALL = 60 * 1024 * 1024
PARAMS = pltpu.CompilerParams(vmem_limit_bytes=32 * 1024 * 1024)


def on_device(tile_flux, inverse_var, kernel_coef, owner_index, offsets, pad_widths):
    row_table, column_table = band_tables()
    owner, corner, pads = owner_index[0].T, offsets[0].T, pad_widths[0].T
    bands = lax.axis_size("band")
    with jax.named_scope("tile_slots"):
        slots = pl.pallas_call(
            slot_kernel,
            out_shape=jax.ShapeDtypeStruct((2, PATCHES, SLOT_ROWS + META_ROWS, TILE), BF16),
            in_specs=[HBM] * 8,
            out_specs=HBM,
            scratch_shapes=[
                pltpu.SMEM((1, TILES_DEV), jnp.int32),
                pltpu.SMEM((2, TILES_DEV), jnp.int32),
                pltpu.SMEM((4, TILES_DEV), jnp.int32),
                pltpu.VMEM((TILES_DEV, 27), BF16),
                pltpu.VMEM((TILES_DEV, 27), F32),
                pltpu.SMEM((TILES_DEV, 27), F32),
                pltpu.VMEM((TILES_DEV, TILE, TILE), BF16),
                pltpu.VMEM((TILES_DEV, TILE, TILE), BF16),
                pltpu.VMEM((TILE, FILTERS * TILE), BF16),
                pltpu.VMEM((TILE, FILTERS * TILE), BF16),
                pltpu.VMEM((2, 2 * TILE, FILTERS * TILE), F32),
                pltpu.VMEM((2, FILTERS * TILE, 2 * TILE), BF16),
                pltpu.VMEM((TILES_DEV, 2, TILE, TILE), F32),
                pltpu.VMEM((TILES_DEV, 2, TILE, TILE), BF16),
                pltpu.VMEM((2, PATCHES, META_ROWS, TILE), BF16),
                pltpu.SemaphoreType.DMA((9,)),
                pltpu.SemaphoreType.DMA((1 + TILES_DEV,)),
            ],
            compiler_params=pltpu.CompilerParams(vmem_limit_bytes=VMEM_ALL),
        )(
            owner,
            corner,
            pads,
            kernel_coef[0],
            tile_flux[0],
            inverse_var[0],
            jnp.asarray(row_table),
            jnp.asarray(column_table),
        )
    slots = slots.reshape((2 * PATCHES,) + slots.shape[2:])
    blocks = [
        [z * PATCHES + patch for z in (low, low + 1) for patch in range(PATCHES)]
        for low in range(0, STRIPS, 2)
    ]
    slots_got = lax.all_to_all(
        slots, ("group", "patch"), 0, 0, tiled=True, axis_index_groups=blocks
    )
    meta = slots_got[:, SLOT_ROWS : SLOT_ROWS + 8, 0].astype(jnp.int32)
    with jax.named_scope("strip_images"):
        kept, sent = pl.pallas_call(
            scatter_kernel,
            out_shape=(
                jax.ShapeDtypeStruct((QUARTER, 2, STRIP, PATCH_SIDE), F32),
                jax.ShapeDtypeStruct((QUARTER, 2, STRIP, PATCH_SIDE), BF16),
            ),
            in_specs=[SMEM, VMEM],
            out_specs=(VMEM, VMEM),
            scratch_shapes=[pltpu.VMEM((2, COL_BLOCKS + 1, PATCH_SIDE // 2, TILE), F32)],
            compiler_params=PARAMS,
        )(meta, slots_got)
    pairs = []
    for z in range(STRIPS):
        for patch in range(PATCHES):
            shift = 2 if (z >> 1) % 2 == patch % 2 else -2
            pairs.append((z * PATCHES + patch, (z + shift) % STRIPS * PATCHES + patch))
    got = lax.ppermute(sent, ("group", "patch"), pairs)
    with jax.named_scope("quad_sums"):
        quads = pl.pallas_call(
            quad_kernel,
            out_shape=(jax.ShapeDtypeStruct((2, STRIP, PATCH_SIDE), F32),)
            + (jax.ShapeDtypeStruct((2, STRIP, PATCH_SIDE), BF16),) * (QUARTER - 1),
            in_specs=[VMEM, VMEM],
            out_specs=(VMEM,) * QUARTER,
            compiler_params=PARAMS,
        )(kept, got)
    strips_got = [quads[0]]
    for step in (2,1,3):
        ring = [(z, (z + 4 * step) % STRIPS) for z in range(STRIPS)]
        strips_got.append(lax.ppermute(quads[step], "group", ring))
    with jax.named_scope("strip_sums"):
        coadd, chi_copies = pl.pallas_call(
            reduce_kernel,
            out_shape=(
                jax.ShapeDtypeStruct((STRIP, PATCH_SIDE), F32),
                jax.ShapeDtypeStruct((bands, STRIP, PATCH_SIDE), BF16),
            ),
            in_specs=[VMEM] * QUARTER,
            out_specs=(VMEM, VMEM),
            compiler_params=PARAMS,
        )(*strips_got)
    chi_parts = lax.all_to_all(chi_copies, "band", 0, 0, tiled=True)
    with jax.named_scope("chi_sum"):
        coadd, chi = pl.pallas_call(
            chi_kernel,
            out_shape=(jax.ShapeDtypeStruct((STRIP, PATCH_SIDE), F32),) * 2,
            in_specs=[VMEM, VMEM],
            out_specs=(VMEM, VMEM),
            compiler_params=PARAMS,
        )(coadd, chi_parts)
    return (coadd[None, None], chi[None])


def solution(mesh):
    return jax.shard_map(
        on_device,
        mesh=mesh,
        in_specs=(
            P("band", ("group", "patch"), None, None),
            P("band", ("group", "patch"), None, None),
            P("band", ("group", "patch"), None),
            P("band", ("group", "patch"), None),
            P("band", ("group", "patch"), None),
            P("band", ("group", "patch"), None),
        ),
        out_specs=(P("band", "patch", "group", None), P("patch", "group", None)),
        check_vma=False,
    )
```

```python
import jax
import jax.numpy as jnp
import ml_dtypes
import numpy as np
from jax import lax
from jax.experimental import pallas as pl
from jax.experimental.pallas import tpu as pltpu
from jax.sharding import PartitionSpec as P

PATCH_SIDE = 512
TILE = 128
TILES_DEV = 8
PATCHES = 8
CAP = 2
SPREADS = (0.7, 1.5, 3.0)
DEGREES = (4, 2, 2)
REACH = 10
STARTS = (0, 5, 8)
FILTERS = 11
META_ROWS = 16
SLOT_ROWS = 2 * CAP * 64
STRIP = 32
STRIPS = PATCH_SIDE // STRIP
QUARTER = STRIPS // 4
COL_BLOCKS = PATCH_SIDE // TILE
F32 = jnp.float32
BF16 = jnp.bfloat16


def basis_filters():
    offsets_axis = np.arange(-REACH, REACH + 1) * 1.0
    filters = []
    for spread_value, degree in zip(SPREADS, DEGREES):
        profile = np.exp(-(offsets_axis**2) / (2.0 * spread_value * spread_value))
        profile = profile / profile.sum()
        for exponent in range(degree + 1):
            filters.append(profile * (offsets_axis / REACH) ** exponent)
    return np.stack(filters)


def band_tables():
    filters = basis_filters()
    source = np.arange(TILE)[:, None]
    target = np.arange(TILE)[None, :]
    shift_table = target - source
    inside = np.abs(shift_table) <= REACH
    picked = filters[:, np.clip(shift_table + REACH, 0, 2 * REACH)] * inside
    row_table = np.transpose(picked, (1, 0, 2)).reshape(TILE, FILTERS * TILE)
    column_table = np.transpose(picked, (2, 0, 1)).reshape(TILE, FILTERS * TILE)
    half = lambda table: table.astype(np.float32).astype(ml_dtypes.bfloat16)
    return half(row_table), half(column_table)


def term_list():
    terms = [[] for _ in range(FILTERS)]
    counter = 0
    for family, degree in enumerate(DEGREES):
        for along_x in range(degree + 1):
            for along_y in range(degree + 1 - along_x):
                terms[STARTS[family] + along_y].append((STARTS[family] + along_x, counter))
                counter += 1
    return terms


TERM_LIST = term_list()


def slots_of(owner_ref, offsets_ref):
    patches = [owner_ref[0, tile] for tile in range(TILES_DEV)]
    codes = [(1 << 16) + (offsets_ref[0, t] << 8) + offsets_ref[1, t] for t in range(TILES_DEV)]
    slots = []
    for tile in range(TILES_DEV):
        seen = jnp.int32(0)
        for other in range(tile):
            seen = seen + jnp.where(patches[other] == patches[tile], codes[other], 0)
        slots.append((patches[tile], seen >> 16, (seen >> 8) & 255, seen & 255))
    return slots


def first_row(row_offset, parity):
    row = row_offset * 8
    return (row >> 6) * STRIP + jnp.clip((row & 63) - STRIP * parity, 0, STRIP)


def rows_of_parity(row_offset, parity):
    ahead = (4 * parity - row_offset) & 7
    cut = jnp.where(ahead > 4, 8 - ahead, 0)
    start = jnp.where(ahead > 4, 0, ahead * 8)
    return [pl.multiple_of(start + 8 * i + (((cut + i) >> 2) << 5), 8) for i in range(4)]


def masked_weight(var_tile, pads_ref, tile):
    line_y = lax.broadcasted_iota(jnp.int32, (TILE, TILE), 0)
    line_x = lax.broadcasted_iota(jnp.int32, (TILE, TILE), 1)
    inside = (
        (line_y >= pads_ref[0, tile])
        & (line_y < TILE - pads_ref[1, tile])
        & (line_x >= pads_ref[2, tile])
        & (line_x < TILE - pads_ref[3, tile])
    )
    return jnp.where(inside, var_tile.astype(F32), 0.0)


def slot_kernel(
    owner_hbm, offsets_hbm, pads_hbm, coef_hbm, flux_hbm, var_hbm, row_hbm, col_hbm, out_hbm,
    owner_ref, offsets_ref, pads_ref, coef_half, coef_full, coef_ref, flux_ref, var_ref, row_ref,
    col_ref, rowpass, mixed, whole, halves, metas, sems, out_sems,
):
    pairs = (
        (owner_hbm, owner_ref),
        (offsets_hbm, offsets_ref),
        (coef_hbm, coef_half),
        (row_hbm, row_ref),
        (flux_hbm, flux_ref),
        (pads_hbm, pads_ref),
        (col_hbm, col_ref),
        (var_hbm, var_ref),
    )
    copies = [pltpu.make_async_copy(a, b, sems.at[i]) for i, (a, b) in enumerate(pairs)]
    for copy in copies:
        copy.start()
    metas[...] = jnp.zeros_like(metas)
    line = lax.broadcasted_iota(jnp.int32, (META_ROWS, TILE), 1)
    for copy in copies[:3]:
        copy.wait()
    coef_full[...] = coef_half[...].astype(F32)
    spread = pltpu.make_async_copy(coef_full, coef_ref, sems.at[len(pairs)])
    spread.start()
    slots = slots_of(owner_ref, offsets_ref)
    for tile in range(TILES_DEV):
        patch, rank, row_before, col_before = slots[tile]
        row_now, col_now = offsets_ref[0, tile], offsets_ref[1, tile]
        second = rank > 0
        entry = {
            0: jnp.int32(1),
            1: jnp.where(second, row_before, row_now),
            2: jnp.where(second, col_before, col_now),
            4: rank,
            5: jnp.where(second, row_now, 0),
            6: jnp.where(second, col_now, 0),
        }
        meta = jnp.zeros((META_ROWS, TILE), jnp.int32)
        for i, value in entry.items():
            meta = jnp.where(line == i, value, meta)
        meta = meta.astype(F32).astype(BF16)
        for parity in range(2):
            metas[parity, patch] = meta
    sent = [
        pltpu.make_async_copy(metas, out_hbm.at[:, :, pl.ds(SLOT_ROWS, META_ROWS), :], out_sems.at[0])
    ]
    sent[0].start()
    copies[3].wait()
    copies[4].wait()
    def row_pass(pair):
        tiles = flux_ref[2 * pair : 2 * pair + 2].reshape(2 * TILE, TILE)
        rowpass[pair % 2] = jnp.dot(tiles, row_ref[...], preferred_element_type=F32)

    def mix(pair):
        side = pair % 2
        for part in range(2):
            coefs = [coef_ref[2 * pair + part, k] for k in range(27)]
            for block in range(0, TILE, 16):
                rows = slice(part * TILE + block, part * TILE + block + 16)
                lines = [rowpass[side, rows, f * TILE : (f + 1) * TILE] for f in range(FILTERS)]
                for g in range(FILTERS):
                    total = None
                    for f, k in TERM_LIST[g]:
                        term = lines[f] * coefs[k]
                        total = term if total is None else total + term
                    mixed[side, g * TILE + block : g * TILE + block + 16,
                          part * TILE : (part + 1) * TILE] = total.astype(BF16)

    def column_pass(pair):
        return jnp.dot(col_ref[...], mixed[pair % 2], preferred_element_type=F32)

    def finish(pair, matched):
        for part in range(2):
            tile = 2 * pair + part
            patch, rank = slots[tile][:2]
            weight = masked_weight(var_ref[tile], pads_ref, tile)
            whole[tile, 0] = weight * matched[:, part * TILE : (part + 1) * TILE]
            whole[tile, 1] = weight
            for parity in range(2):
                taken = rows_of_parity(offsets_ref[0, tile], parity)
                taken = taken + [pl.multiple_of(row + 64, 8) for row in taken]
                for image in range(2):
                    rows = [whole[tile, image, pl.ds(row, 8), :] for row in taken]
                    halves[tile, parity, image * 64 : (image + 1) * 64, :] = jnp.concatenate(
                        rows, axis=0
                    ).astype(BF16)
            start = pl.multiple_of(rank * TILE, TILE)
            copy = pltpu.make_async_copy(
                halves.at[tile],
                out_hbm.at[:, patch, pl.ds(start, TILE), :],
                out_sems.at[1 + tile],
            )
            copy.start()
            sent.append(copy)

    row_pass(0)
    spread.wait()
    for copy in copies[5:]:
        copy.wait()
    matched = None
    for pair in range(TILES_DEV // 2):
        if pair + 1 < TILES_DEV // 2:
            row_pass(pair + 1)
        mix(pair)
        if pair > 0:
            finish(pair - 1, matched)
        matched = column_pass(pair)
    finish(TILES_DEV // 2 - 1, matched)
    for copy in sent:
        copy.wait()


def scatter_kernel(meta_ref, slots_ref, keep_ref, send_ref, images):
    images[...] = jnp.zeros_like(images)
    parity = lax.rem(lax.axis_index("group"), 2)
    lane = lax.broadcasted_iota(jnp.int32, (64, TILE), 1)
    for rank in range(CAP):
        for source in range(2 * PATCHES):
            filled = meta_ref[source, rank * 4] != 0
            row = first_row(meta_ref[source, rank * 4 + 1], parity)
            row = pl.multiple_of(row, 8)
            column = meta_ref[source, rank * 4 + 2] * 8
            block = column >> 7
            shift = column & (TILE - 1)
            right = lane >= jnp.where(filled, shift, TILE)
            left = lane < jnp.where(filled, shift, 0)
            for image in range(2):
                start = rank * TILE + image * 64
                half = slots_ref[source, start : start + 64, :].astype(F32)
                turned = pltpu.roll(half, shift, 1)
                place = (image, block, pl.ds(row, 64), slice(None))
                images[place] += jnp.where(right, turned, 0.0)
                place = (image, block + 1, pl.ds(row, 64), slice(None))
                images[place] += jnp.where(left, turned, 0.0)

    own = (lax.axis_index("group") >> 1) & 1
    for entry in range(QUARTER):
        kept = pl.multiple_of((2 * entry + own) * STRIP, STRIP)
        sent = pl.multiple_of((2 * entry + 1 - own) * STRIP, STRIP)
        for image in range(2):
            for block in range(COL_BLOCKS):
                columns = slice(block * TILE, (block + 1) * TILE)
                keep_ref[entry, image, :, columns] = images[image, block, pl.ds(kept, STRIP), :]
                send_ref[entry, image, :, columns] = images[
                    image, block, pl.ds(sent, STRIP), :
                ].astype(BF16)


def quad_kernel(keep_ref, got_ref, own_ref, *out_refs):
    here = lax.axis_index("group") >> 2
    own_ref[...] = keep_ref[here] + got_ref[here].astype(F32)
    for step, out_ref in enumerate(out_refs, 1):
        entry = (here + step) & (QUARTER - 1)
        out_ref[...] = (keep_ref[entry] + got_ref[entry].astype(F32)).astype(BF16)


def reduce_kernel(own_ref, *refs):
    strip_refs, (coadd_ref, chi_ref) = refs[:-2], refs[-2:]
    flux, weight = own_ref[0], own_ref[1]
    for strip_ref in strip_refs:
        flux = flux + strip_ref[0].astype(F32)
        weight = weight + strip_ref[1].astype(F32)
    coadd = flux / (weight + 1.0)
    coadd_ref[...] = coadd
    chi = (flux * coadd).astype(BF16)
    for band in range(chi_ref.shape[0]):
        chi_ref[band] = chi


def chi_kernel(coadd_ref, parts_ref, coadd_out, chi_out):
    coadd_out[...] = coadd_ref[...]
    total = parts_ref[0].astype(F32)
    for band in range(1, parts_ref.shape[0]):
        total = total + parts_ref[band].astype(F32)
    chi_out[...] = total


SMEM = pl.BlockSpec(memory_space=pltpu.SMEM)
VMEM = pl.BlockSpec(memory_space=pltpu.VMEM)
HBM = pl.BlockSpec(memory_space=pltpu.HBM)
VMEM_ALL = 60 * 1024 * 1024
PARAMS = pltpu.CompilerParams(vmem_limit_bytes=32 * 1024 * 1024)


def on_device(tile_flux, inverse_var, kernel_coef, owner_index, offsets, pad_widths):
    row_table, column_table = band_tables()
    owner, corner, pads = owner_index[0].T, offsets[0].T, pad_widths[0].T
    bands = lax.axis_size("band")
    with jax.named_scope("tile_slots"):
        slots = pl.pallas_call(
            slot_kernel,
            out_shape=jax.ShapeDtypeStruct((2, PATCHES, SLOT_ROWS + META_ROWS, TILE), BF16),
            in_specs=[HBM] * 8,
            out_specs=HBM,
            scratch_shapes=[
                pltpu.SMEM((1, TILES_DEV), jnp.int32),
                pltpu.SMEM((2, TILES_DEV), jnp.int32),
                pltpu.SMEM((4, TILES_DEV), jnp.int32),
                pltpu.VMEM((TILES_DEV, 27), BF16),
                pltpu.VMEM((TILES_DEV, 27), F32),
                pltpu.SMEM((TILES_DEV, 27), F32),
                pltpu.VMEM((TILES_DEV, TILE, TILE), BF16),
                pltpu.VMEM((TILES_DEV, TILE, TILE), BF16),
                pltpu.VMEM((TILE, FILTERS * TILE), BF16),
                pltpu.VMEM((TILE, FILTERS * TILE), BF16),
                pltpu.VMEM((2, 2 * TILE, FILTERS * TILE), F32),
                pltpu.VMEM((2, FILTERS * TILE, 2 * TILE), BF16),
                pltpu.VMEM((TILES_DEV, 2, TILE, TILE), F32),
                pltpu.VMEM((TILES_DEV, 2, TILE, TILE), BF16),
                pltpu.VMEM((2, PATCHES, META_ROWS, TILE), BF16),
                pltpu.SemaphoreType.DMA((9,)),
                pltpu.SemaphoreType.DMA((1 + TILES_DEV,)),
            ],
            compiler_params=pltpu.CompilerParams(vmem_limit_bytes=VMEM_ALL),
        )(
            owner,
            corner,
            pads,
            kernel_coef[0],
            tile_flux[0],
            inverse_var[0],
            jnp.asarray(row_table),
            jnp.asarray(column_table),
        )
    slots = slots.reshape((2 * PATCHES,) + slots.shape[2:])
    blocks = [
        [z * PATCHES + patch for z in (low, low + 1) for patch in range(PATCHES)]
        for low in range(0, STRIPS, 2)
    ]
    slots_got = lax.all_to_all(
        slots, ("group", "patch"), 0, 0, tiled=True, axis_index_groups=blocks
    )
    meta = slots_got[:, SLOT_ROWS, :8].astype(jnp.int32)
    with jax.named_scope("strip_images"):
        kept, sent = pl.pallas_call(
            scatter_kernel,
            out_shape=(
                jax.ShapeDtypeStruct((QUARTER, 2, STRIP, PATCH_SIDE), F32),
                jax.ShapeDtypeStruct((QUARTER, 2, STRIP, PATCH_SIDE), BF16),
            ),
            in_specs=[SMEM, VMEM],
            out_specs=(VMEM, VMEM),
            scratch_shapes=[pltpu.VMEM((2, COL_BLOCKS + 1, PATCH_SIDE // 2, TILE), F32)],
            compiler_params=PARAMS,
        )(meta, slots_got)
    pairs = []
    for z in range(STRIPS):
        for patch in range(PATCHES):
            shift = 2 if (z >> 1) % 2 == patch % 2 else -2
            pairs.append((z * PATCHES + patch, (z + shift) % STRIPS * PATCHES + patch))
    got = lax.ppermute(sent, ("group", "patch"), pairs)
    with jax.named_scope("quad_sums"):
        quads = pl.pallas_call(
            quad_kernel,
            out_shape=(jax.ShapeDtypeStruct((2, STRIP, PATCH_SIDE), F32),)
            + (jax.ShapeDtypeStruct((2, STRIP, PATCH_SIDE), BF16),) * (QUARTER - 1),
            in_specs=[VMEM, VMEM],
            out_specs=(VMEM,) * QUARTER,
            compiler_params=PARAMS,
        )(kept, got)
    strips_got = [quads[0]]
    for step in (2,1,3):
        ring = [(z, (z + 4 * step) % STRIPS) for z in range(STRIPS)]
        strips_got.append(lax.ppermute(quads[step], "group", ring))
    with jax.named_scope("strip_sums"):
        coadd, chi_copies = pl.pallas_call(
            reduce_kernel,
            out_shape=(
                jax.ShapeDtypeStruct((STRIP, PATCH_SIDE), F32),
                jax.ShapeDtypeStruct((bands, STRIP, PATCH_SIDE), BF16),
            ),
            in_specs=[VMEM] * QUARTER,
            out_specs=(VMEM, VMEM),
            compiler_params=PARAMS,
        )(*strips_got)
    chi_parts = lax.all_to_all(chi_copies, "band", 0, 0, tiled=True)
    with jax.named_scope("chi_sum"):
        coadd, chi = pl.pallas_call(
            chi_kernel,
            out_shape=(jax.ShapeDtypeStruct((STRIP, PATCH_SIDE), F32),) * 2,
            in_specs=[VMEM, VMEM],
            out_specs=(VMEM, VMEM),
            compiler_params=PARAMS,
        )(coadd, chi_parts)
    return (coadd[None, None], chi[None])


def solution(mesh):
    return jax.shard_map(
        on_device,
        mesh=mesh,
        in_specs=(
            P("band", ("group", "patch"), None, None),
            P("band", ("group", "patch"), None, None),
            P("band", ("group", "patch"), None),
            P("band", ("group", "patch"), None),
            P("band", ("group", "patch"), None),
            P("band", ("group", "patch"), None),
        ),
        out_specs=(P("band", "patch", "group", None), P("patch", "group", None)),
        check_vma=False,
    )
```
